512 devices in a mesh: gx: 8 (over y), gy: 8 (over z), gz: 8 (over x, core).
Axes of the slice: x: 4, y: 8, z: 8, core: 2. Of those that a mesh axis runs over, the one named last changes fastest.
Arguments:
- divergence: float32 [128, 128, 1024], P('gz', 'gx', 'gy'), may hold values from -6 to 6
- pressure_prev: float32 [128, 128, 1024], P('gz', 'gx', 'gy'), may hold values from -6 to 6
Outputs:
- pressure: float32 [128, 128, 1024], P('gz', 'gx', 'gy')
- residual: float32 [128, 128, 1024], P('gz', 'gx', 'gy')
- coarse_correction: float32 [4, 4, 32], replicated
The draws below stay inside these ranges and needn't reach their ends.
All inputs are finite; a program needn't handle non-finite values.
Results may differ from the reference program's by a relative error of at most 0.0004.
Values sent between devices are 32-bit elements; how exact they have to be, the bound alone decides.
A program may use at most 64 MiB of HBM per device.

```python
import jax
import jax.numpy as jnp

LEVELS = 6
NX = 128
NY = 1024
NZ = 128


def draw_divergence(key, part):
    key = jax.random.fold_in(key, 3)
    first_key = jax.random.fold_in(key, 0)
    return jax.random.truncated_normal(first_key, -6.0, 6.0, (NZ, NX, NY), jnp.float32)


def level_of(rng, shape, shards, smallest, high):
    def one(position, shards_of):
        steps = jax.random.uniform(jax.random.fold_in(jax.random.fold_in(rng, 6), position), (shards_of,), jnp.float32, smallest / len(shards), high / len(shards))
        return jnp.repeat(jnp.exp(steps), shape[position] // shards_of).reshape((-1,) + (1,) * (len(shape) - position - 1))

    gain = one(*shards[0])
    for cut in shards[1:]:
        gain = gain * one(*cut)
    return gain


def bell_draw(key, shape, deviation, bound, cuts=(), kind=jnp.bfloat16):
    entries = deviation * jax.random.normal(key, shape, jnp.float32)
    if cuts:
        entries = entries * level_of(key, shape, cuts, -0.22, 0.18)
    return jnp.clip(entries, -bound, bound).astype(kind)


def setup_inputs(seed: int = 0) -> dict:
    seeds = jax.random.split(jax.random.key(seed), 3)
    return {
        "divergence": draw_divergence(jax.random.fold_in(seeds[2], 71), 0),
        "pressure_prev": bell_draw(seeds[1], (NZ, NX, NY), 1.0, 6.0, ((0, 8), (1, 8), (2, 8)), jnp.float32),
    }


first_scale = 1.0 / 7.5
rho_one = 1.0 / (2.0 * (5.0 / 3.0) - 0.6)
carry_coef = 0.6 * rho_one
fresh_coef = 2.0 * rho_one / (0.75 * 6.0)


def stencil(values):
    padded = jnp.pad(values, 1)
    beside = padded[2:, 1:-1, 1:-1] + padded[:-2, 1:-1, 1:-1]
    beside = beside + padded[1:-1, 2:, 1:-1] + padded[1:-1, :-2, 1:-1]
    beside = beside + padded[1:-1, 1:-1, 2:] + padded[1:-1, 1:-1, :-2]
    return 6.0 * values - beside


def smooth_pass(iterate, source, apply_op, from_zero):
    residue = source if from_zero else source - apply_op(iterate)
    update = residue * first_scale
    iterate = update if from_zero else iterate + update
    residue = source - apply_op(iterate)
    update = carry_coef * update + fresh_coef * residue
    return iterate + update


def restrict(values):
    shape_a, shape_b, shape_c = values.shape
    blocks = values.reshape(shape_a // 2, 2, shape_b // 2, 2, shape_c // 2, 2)
    return 0.5 * jnp.sum(blocks, axis=(1, 3, 5))


def prolong(values):
    shape_a, shape_b, shape_c = values.shape
    spread = jnp.broadcast_to(values[:, None, :, None, :, None], (shape_a, 2, shape_b, 2, shape_c, 2))
    return spread.reshape(2 * shape_a, 2 * shape_b, 2 * shape_c)


def vcycle(level_num, iterate, source, from_zero):
    iterate = smooth_pass(iterate, source, stencil, from_zero)
    coarsest = None
    if level_num < LEVELS - 1:
        residue = source - stencil(iterate)
        coarse, coarsest = vcycle(level_num + 1, None, restrict(residue), True)
        iterate = iterate + prolong(coarse)
    result = smooth_pass(iterate, source, stencil, False)
    if level_num == LEVELS - 1:
        coarsest = result
    return result, coarsest


def reference(divergence, pressure_prev):
    pressure, coarse_correction = vcycle(0, pressure_prev, divergence, False)
    residual = divergence - stencil(pressure)
    return (pressure, residual, coarse_correction)
```

```python
import functools

import jax
import jax.numpy as jnp
from jax import lax
from jax.experimental import pallas as pl
from jax.experimental.pallas import tpu as pltpu
from jax.sharding import PartitionSpec as P

FIRST = 1.0 / 7.5
RHO = 1.0 / (2.0 * (5.0 / 3.0) - 0.6)
CARRY = 0.6 * RHO
FRESH = 2.0 * RHO / (0.75 * 6.0)
ALPHA = FIRST * (1.0 + CARRY) + FRESH
BETA = FRESH * FIRST
OWN = ALPHA - 6.0 * BETA

LANES = 128
RING = 8

SHIFTS = {
    "x0+": ("gx", 1, 32, 8), "x0-": ("gx", -1, 32, 8),
    "x1+": ("gx", 1, 12, 8), "x1-": ("gx", -1, 12, 8),
    "x2+1": ("gx", 1, 8, 8), "x2-1": ("gx", -1, 8, 8),
    "x2+2": ("gx", 2, 8, 8), "x2-2": ("gx", -2, 8, 8),
    "z0+": ("gz", 1, 9, 32), "z0-": ("gz", -1, 9, 32),
    "z1+": ("gz", 1, 7, 24), "z1-": ("gz", -1, 7, 24),
    "z2+1": ("gz", 1, 7, 16), "z2-1": ("gz", -1, 7, 16),
    "z2+2": ("gz", 2, 3, 16), "z2-2": ("gz", -2, 3, 16),
    "y0+": ("gy", 1, 4, 32), "y0-": ("gy", -1, 4, 32),
    "y1+": ("gy", 1, 2, 24), "y1-": ("gy", -1, 2, 24),
    "y2+": ("gy", 1, 1, 16), "y2-": ("gy", -1, 1, 16),
    "y3+": ("gy", 1, 4, 16), "y3-": ("gy", -1, 4, 16),
}
GATHERS = {"gx3": ("gx", 8), "gz3": ("gz", 16), "gy4": ("gy", 8)}


def iota(shape, dim):
    return lax.broadcasted_iota(jnp.int32, shape, dim)


def number(cond):
    return jnp.where(cond, 1.0, 0.0).astype(jnp.float32)


def dot(a, b):
    return jnp.dot(a, b, precision=lax.Precision.HIGHEST, preferred_element_type=jnp.float32)


def select_matrix(shape, hit, value=1.0):
    return number(hit(iota(shape, 0), iota(shape, 1))) * value


def rows_of(stacked, rows):
    return [stacked[i * rows:(i + 1) * rows] for i in range(stacked.shape[0] // rows)]


def lanes_of(stacked):
    return [stacked[:, i * LANES:(i + 1) * LANES] for i in range(stacked.shape[1] // LANES)]


def right(planes, matrix):
    return rows_of(dot(jnp.concatenate(planes, axis=0), matrix), planes[0].shape[0])


def left(matrix, planes):
    return lanes_of(dot(matrix, jnp.concatenate(planes, axis=1)))


def total(terms):
    terms = [t for t in terms if t is not None]
    out = terms[0]
    for t in terms[1:]:
        out = out + t
    return out


class Field:
    def __init__(self, lo, hi, make):
        self.lo, self.hi, self.make, self.have = lo, hi, make, {}

    def __call__(self, z):
        if z < self.lo or z > self.hi:
            return None
        if z not in self.have:
            self.have[z] = self.make(z)
        return self.have[z]


def field_of(lo, planes):
    return Field(lo, lo + len(planes) - 1, lambda z: planes[z - lo])


class Math:
    def __init__(self, env):
        self.env = env
        self.iz, self.ix, self.iy = env.position

    def roll(self, v, shift, axis):
        shift = shift % v.shape[axis]
        return v if shift == 0 else self.env.roll(v, shift, axis)

    def place_rows(self, v, at, rows):
        pad = jnp.zeros((rows - v.shape[0],) + v.shape[1:], v.dtype)
        return self.roll(jnp.concatenate([v, pad], axis=0), at, 0)

    def take_rows(self, v, at, rows):
        return self.roll(v, -at, 0)[:rows]

    def mask(self, level, rows, row_off, lanes, own_y):
        nz, nx, ny = 16 >> level, 16 >> level, 128 >> level
        x = iota((rows, lanes), 0) - row_off + self.ix * nx
        lane = iota((rows, lanes), 1)
        y = jnp.where(lane < (own_y + lanes) // 2, lane, lane - lanes) + self.iy * ny
        flat = number((x >= 0) & (x < 128 >> level) & (y >= 0) & (y < 1024 >> level))

        def make(z):
            if 0 <= z < nz:
                return flat
            at = self.iz * nz + z
            return flat * number((at >= 0) & (at < 128 >> level))

        return Field(-16, 32, make)

    def beside(self, f, z):
        v = f(z)
        terms = [f(z - 1), f(z + 1)]
        if v is not None:
            terms += [self.roll(v, 1, 0), self.roll(v, -1, 0), self.roll(v, 1, 1), self.roll(v, -1, 1)]
        return total(terms)

    def correction(self, r, mask, lo, hi):
        def make(z):
            v = r(z)
            near = BETA * self.beside(r, z)
            return mask(z) * (near if v is None else OWN * v + near)
        return Field(lo, hi, make)

    def minus_op(self, b, x, mask, lo, hi):
        def make(z):
            out = self.beside(x, z)
            if x(z) is not None:
                out = out - 6.0 * x(z)
            if b(z) is not None:
                out = out + b(z)
            return mask(z) * out
        return Field(lo, hi, make)

    def slots(self, rows, start):
        lane = (iota((rows, LANES), 1) - start) % LANES
        return number(lane < 8)

    def pack(self, planes, start):
        rows = planes[0].shape[0]
        tiles = []
        for g in range(0, len(planes), 16):
            tile = None
            for w, plane in enumerate(planes[g:g + 16]):
                part = self.slots(rows, 8 * w) * self.roll(plane, 8 * w - start, 1)
                tile = part if tile is None else tile + part
            tiles.append(tile)
        return tiles

    def unpack(self, tiles, count, start):
        keep = self.slots(tiles[0].shape[0], start)
        return [keep * self.roll(tiles[i // 16], start - 8 * (i % 16), 1) for i in range(count)]


def cycle(env, x_own, b_own):
    m = Math(env)
    iz, ix, iy = env.position
    zeros = lambda *s: jnp.zeros(s, jnp.float32)

    mask0 = m.mask(0, 24, 4, 256, 128)
    put0 = lambda v: jnp.concatenate([m.place_rows(v, 4, 24), zeros(24, LANES)], axis=1)
    xc = Field(0, 15, lambda z: put0(x_own[z]))
    bc = Field(0, 15, lambda z: put0(b_own[z]))
    r0 = m.minus_op(bc, xc, mask0, -1, 16)
    u0 = m.correction(r0, mask0, -2, 17)
    p0 = m.minus_op(r0, u0, mask0, -3, 18)
    coarse = [total([p0(2 * z), p0(2 * z + 1)]) for z in range(-2, 10)]
    coarse = right(coarse, select_matrix((256, 128), lambda a, c: (a >> 1) == c, 0.5))
    coarse = left(select_matrix((16, 24), lambda a, c: (c >> 1) + 2 == a), coarse)
    mask1c = m.mask(1, 16, 4, 128, 64)
    b1c = field_of(-2, [mask1c(z) * v for z, v in zip(range(-2, 10), coarse)])

    u1 = m.correction(b1c, mask1c, -3, 10)
    p1 = m.minus_op(b1c, u1, mask1c, -4, 11)
    coarse = [total([p1(2 * z), p1(2 * z + 1)]) for z in range(-2, 6)]
    half = select_matrix((128, 128), lambda a, c: (a >> 1) + jnp.where(a >= 96, 64, 0) == c, 0.5)
    coarse = right(coarse, half)
    halve_rows = select_matrix((8, 16), lambda a, c: (c >> 1) == a)
    coarse = left(halve_rows, coarse)
    mask2e = m.mask(2, 8, 2, 128, 32)
    b2c = [mask2e(z) * v for z, v in zip(range(-2, 6), coarse)]

    mask2c = m.mask(2, 16, 4, 128, 32)
    b2p = field_of(-2, [m.place_rows(v, 2, 16) for v in b2c])
    u2 = m.correction(b2p, mask2c, -3, 6)
    p2 = m.minus_op(b2p, u2, mask2c, -4, 7)
    coarse = [total([p2(2 * z), p2(2 * z + 1)]) for z in range(-2, 4)]
    half = select_matrix((128, 128), lambda a, c: (jnp.where(a < 80, a, a - 128) >> 1) + 2 == c, 0.5)
    coarse = left(halve_rows, right(coarse, half))
    b3c = total([m.roll(v, 20 * s, 1) for s, v in enumerate(coarse)])

    env.ready()
    env.gather_send("gx3", b3c)
    for d in (1, -1, 2, -2):
        env.shift_send("x2%+d" % d, b2c)
    env.shift_send("x1+", [m.take_rows(b1c(z), 7, 8) for z in range(-2, 10)])
    env.shift_send("x1-", [m.take_rows(b1c(z), 2, 8) for z in range(-2, 10)])
    env.shift_send("x0+", [v[8:] for v in x_own] + [v[8:] for v in b_own])
    env.shift_send("x0-", [v[:8] for v in x_own] + [v[:8] for v in b_own])

    parts = env.gather_recv("gx3")
    wide = total([m.place_rows(v, 2 * k, 24) for k, v in enumerate(parts)])
    b3x = m.take_rows(wide, 2, 16)

    env.gather_send("gz3", b3x)

    got = {d: env.shift_recv("x2%+d" % d) for d in (1, -1, 2, -2)}
    row8 = iota((8, LANES), 0)
    low, high = number(row8 < 4), number(row8 >= 4)
    b2x = []
    for i in range(8):
        lo = got[1][i] + low * m.roll(got[2][i], 4, 0)
        hi = got[-1][i] + high * m.roll(got[-2][i], 4, 0)
        b2x.append(jnp.concatenate([lo, hi], axis=0) + m.place_rows(b2c[i], 4, 16))
    env.shift_send("z2+1", b2x[1:])
    env.shift_send("z2-1", b2x[:7])
    env.shift_send("z2+2", b2x[5:])
    env.shift_send("z2-2", b2x[:3])

    before, after = env.shift_recv("x1+"), env.shift_recv("x1-")
    b1x = [
        m.place_rows(b1c(i - 2), 4, 24) + m.place_rows(before[i], 3, 24) + m.place_rows(after[i], 14, 24)
        for i in range(12)
    ]
    env.shift_send("z1+", b1x[5:])
    env.shift_send("z1-", b1x[:7])

    before, after = env.shift_recv("x0+"), env.shift_recv("x0-")
    own = x_own + b_own
    joined = [jnp.concatenate([before[i], own[i], after[i]], axis=0) for i in range(32)]
    x0x, b0x = joined[:16], joined[16:]
    env.shift_send("z0+", x0x[11:] + b0x[12:])
    env.shift_send("z0-", x0x[:5] + b0x[:4])

    parts = env.gather_recv("gz3")
    lane = iota((16, LANES), 1)
    tiles = []
    for q in range(4):
        tile = None
        for w in range(4):
            z = 4 * q + w
            here = []
            for k in range(RING):
                s = z - 2 * k + 2
                if 0 <= s < 6:
                    here.append(m.roll(parts[k], 32 * w + 6 - 20 * s, 1))
            at = lane - (32 * w + 6)
            part = number((at >= 0) & (at < 20)) * total(here)
            tile = part if tile is None else tile + part
        tiles.append(tile)
    row16, lane512 = iota((16, 512), 0), iota((16, 512), 1)
    slot = lane512 & 31
    y3 = slot - 8 + 16 * iy
    mask3 = number((y3 >= 0) & (y3 < 128))
    not_first, not_last = number(row16 > 0), number(row16 < 15)
    not_bottom, not_top = number(lane512 >= 32), number(lane512 < 480)

    def beside3(v):
        out = not_first * m.roll(v, 1, 0) + not_last * m.roll(v, -1, 0)
        out = out + not_bottom * m.roll(v, 32, 1) + not_top * m.roll(v, -32, 1)
        return out + m.roll(v, 1, 1) + m.roll(v, -1, 1)

    correction3 = lambda r: mask3 * (OWN * r + BETA * beside3(r))
    minus_op3 = lambda b, x: mask3 * (b - 6.0 * x + beside3(x))

    b3s = mask3 * jnp.concatenate(tiles, axis=1)
    p3 = minus_op3(b3s, correction3(b3s))
    gather_lanes = select_matrix((512, 128), lambda a, c: 16 * (a >> 6) + ((a & 31) >> 1) == c, 0.5)
    b4c = dot(halve_rows, dot(p3, gather_lanes))

    env.gather_send("gy4", b4c)
    env.shift_send("y3+", lanes_of(b3s))
    env.shift_send("y3-", lanes_of(b3s))

    got = {d: env.shift_recv("z2%+d" % d) for d in (1, -1, 2, -2)}
    b2w = []
    for z in range(-5, 9):
        here = []
        if -2 <= z <= 5:
            here.append(b2x[z + 2])
        if z <= 1:
            here.append(got[1][z + 5])
        if z >= 2:
            here.append(got[-1][z - 2])
        if z <= -3:
            here.append(got[2][z + 5])
        if z >= 6:
            here.append(got[-2][z - 6])
        b2w.append(total(here))
    env.shift_send("y2+", m.pack(b2w, 27))
    env.shift_send("y2-", m.pack(b2w, 126))

    before, after = env.shift_recv("z1+"), env.shift_recv("z1-")
    b1w = []
    for z in range(-5, 13):
        here = []
        if -2 <= z <= 9:
            here.append(b1x[z + 2])
        if z <= 1:
            here.append(before[z + 5])
        if z >= 6:
            here.append(after[z - 6])
        b1w.append(total(here))
    env.shift_send("y1+", m.pack(b1w, 59))
    env.shift_send("y1-", m.pack(b1w, 126))

    before, after = env.shift_recv("z0+"), env.shift_recv("z0-")
    x0w = before[:5] + x0x + after[:5]
    b0w = before[5:] + b0x + after[5:]
    env.shift_send("y0+", m.pack(x0w, 120) + m.pack(b0w, 120))
    env.shift_send("y0-", m.pack(x0w, 0) + m.pack(b0w, 0))

    parts = env.gather_recv("gy4")
    row, lane = iota((8, LANES), 0), iota((8, LANES), 1)
    keep = []
    for j in range(RING):
        at = lane - (8 * j - 4)
        keep.append(number((at >= 0) & (at < 16) & (lane < 64)))
    b4 = field_of(0, [
        total([keep[j] * m.roll(parts[j], 8 * j - 4 - 16 * z, 1) for j in range(RING)]) for z in range(8)
    ])
    mask4 = number(lane < 64)
    first8, last8 = number(row > 0), number(row < 7)

    def beside4(f, z):
        v = f(z)
        return total([
            f(z - 1), f(z + 1), first8 * m.roll(v, 1, 0), last8 * m.roll(v, -1, 0), m.roll(v, 1, 1), m.roll(v, -1, 1)
        ])

    def correction4(r):
        return Field(0, 7, lambda z: mask4 * (OWN * r(z) + BETA * beside4(r, z)))

    def minus_op4(b, x):
        return Field(0, 7, lambda z: mask4 * (b(z) - 6.0 * x(z) + beside4(x, z)))

    u4 = correction4(b4)
    p4 = minus_op4(b4, u4)
    half = select_matrix((128, 128), lambda a, c: ((a >> 1) == c) & (a < 64), 0.5)
    coarse = jnp.concatenate([p4(2 * z) + p4(2 * z + 1) for z in range(4)], axis=0)
    b5 = dot(select_matrix((16, 32), lambda a, c: (c >> 3) * 4 + ((c & 7) >> 1) == a), dot(coarse, half))

    row, lane = iota((16, LANES), 0), iota((16, LANES), 1)
    mask5 = number(lane < 32)
    first5, last5 = number((row & 3) > 0), number((row & 3) < 3)
    bottom5, top5 = number(row >= 4), number(row < 12)

    def beside5(v):
        out = first5 * m.roll(v, 1, 0) + last5 * m.roll(v, -1, 0)
        out = out + bottom5 * m.roll(v, 4, 0) + top5 * m.roll(v, -4, 0)
        return out + m.roll(v, 1, 1) + m.roll(v, -1, 1)

    u5 = mask5 * (OWN * b5 + BETA * beside5(b5))
    p5 = mask5 * (b5 - 6.0 * u5 + beside5(u5))
    e5 = u5 + mask5 * (OWN * p5 + BETA * beside5(p5))
    env.coarse_out(e5)

    double = select_matrix((128, 128), lambda a, c: (a == (c >> 1)) & (c < 64))
    wide = dot(select_matrix((32, 16), lambda a, c: (a >> 3) * 4 + ((a & 7) >> 1) == c), dot(e5, double))
    c4 = rows_of(wide, 8)
    c4 = field_of(0, [c4[z // 2] for z in range(8)])
    q4 = minus_op4(p4, c4)
    v4 = correction4(q4)
    e4 = [u4(z) + c4(z) + v4(z) for z in range(8)]

    own_y = select_matrix((128, 128), lambda a, c: (a == 8 * iy + (((c & 31) - 8) >> 1)) & (c < 64))
    planes = right(e4, own_y)
    wide = jnp.concatenate([planes[2 * k] + m.roll(planes[2 * k + 1], 64, 1) for k in range(4)], axis=1)
    c3 = mask3 * dot(select_matrix((16, 8), lambda a, c: (a >> 1) == c), wide)
    before = jnp.concatenate(env.shift_recv("y3+"), axis=1)
    after = jnp.concatenate(env.shift_recv("y3-"), axis=1)
    b3w = b3s + number((slot >= 3) & (slot < 10)) * m.roll(before, -16, 1)
    b3w = mask3 * (b3w + number((slot >= 22) & (slot < 29)) * m.roll(after, 16, 1))
    u3 = correction3(b3w)
    p3 = minus_op3(b3w, u3)
    e3 = u3 + c3 + correction3(minus_op3(p3, c3))

    spread = select_matrix((16, 16), lambda a, c: 2 * ix + ((a - 6) >> 1) == c)
    tiles = lanes_of(dot(spread, e3))
    near = env.window([m.roll(tiles[z // 4], -32 * (z % 4), 1) for z in range(16)])
    y_of = lambda c: jnp.where(c < 80, c, c - 128)
    own_y = select_matrix(
        (128, 128), lambda a, c: (a - 8 == (y_of(c) >> 1)) & (a < 32) & (y_of(c) < 36) & (y_of(c) >= -4))
    near = right(near, own_y)
    c2 = field_of(-4, [near[(z >> 1) + 2] for z in range(-4, 8)])

    def window(level, planes, tag, rows, row_off, lo, own_y, at_low, at_high):
        mask = m.mask(level, rows, row_off, LANES, own_y)
        before = m.unpack(env.shift_recv(tag + "+"), len(planes), at_low)
        after = m.unpack(env.shift_recv(tag + "-"), len(planes), at_high)
        return mask, field_of(lo, [
            mask(lo + i) * (v + before[i] + after[i]) for i, v in enumerate(planes)
        ])

    mask2, b2 = window(2, b2w, "y2", 16, 6, -5, 32, 123, 30)
    u2 = m.correction(b2, mask2, -4, 7)
    p2 = m.minus_op(b2, u2, mask2, -3, 6)
    v2 = m.correction(m.minus_op(p2, c2, mask2, -3, 6), mask2, -2, 5)
    e2 = [u2(z) + mask2(z) * c2(z) + v2(z) for z in range(-2, 6)]

    y_fine = lambda c: jnp.where(c < 96, c, c - 128)
    own_y = select_matrix((128, 128), lambda a, c: y_of(a) == (y_fine(c) >> 1))
    coarse = left(select_matrix((24, 16), lambda a, c: (a >> 1) + 2 == c), e2)
    coarse = right(coarse, own_y)
    c1 = field_of(-4, [coarse[(z >> 1) + 2] for z in range(-4, 12)])
    mask1, b1 = window(1, b1w, "y1", 24, 8, -5, 64, 123, 62)
    u1 = m.correction(b1, mask1, -4, 11)
    p1 = m.minus_op(b1, u1, mask1, -3, 10)
    v1 = m.correction(m.minus_op(p1, c1, mask1, -3, 10), mask1, -2, 9)
    e1 = [u1(z) + mask1(z) * c1(z) + v1(z) for z in range(-2, 10)]

    coarse = left(select_matrix((32, 24), lambda a, c: (a >> 1) + 4 == c), e1)
    coarse = right(coarse, select_matrix((128, 256), lambda a, c: a == (c >> 1)))
    c0 = field_of(-4, [coarse[(z >> 1) + 2] for z in range(-4, 20)])
    mask0 = m.mask(0, 32, 8, 256, 128)
    before, after = env.shift_recv("y0+"), env.shift_recv("y0-")

    def window0(planes, lo, some):
        low = m.unpack(before[some], len(planes), 120)
        high = m.unpack(after[some], len(planes), 0)
        return field_of(lo, [
            mask0(lo + i) * jnp.concatenate([v, low[i] + high[i]], axis=1) for i, v in enumerate(planes)
        ])

    x0 = window0(x0w, -5, slice(0, 2))
    b0 = window0(b0w, -4, slice(2, 4))
    r0 = m.minus_op(b0, x0, mask0, -4, 19)
    u0 = m.correction(r0, mask0, -3, 18)
    p0 = m.minus_op(r0, u0, mask0, -2, 17)
    q0 = m.minus_op(p0, c0, mask0, -2, 17)
    v0 = m.correction(q0, mask0, -1, 16)
    left_over = m.minus_op(q0, v0, mask0, 0, 15)
    inner = lambda v: v[8:24, :LANES]
    for z in range(16):
        env.fine_out(z, x_own[z] + inner(u0(z)) + inner(c0(z)) + inner(v0(z)), inner(left_over(z)))


class KernelEnv:
    def __init__(self, refs):
        self.refs = refs
        self.position = tuple(lax.axis_index(a) for a in ("gz", "gx", "gy"))
        self.at = dict(zip(("gz", "gx", "gy"), self.position))
        self.started = []
        self.barrier = pltpu.get_barrier_semaphore()
        for axis in ("gx", "gz", "gy"):
            for d in range(1, RING):
                pl.semaphore_signal(
                    self.barrier, inc=1, device_id={axis: self.peer(axis, d)}, device_id_type=pl.DeviceIdType.MESH)

    def peer(self, axis, d):
        return lax.rem(self.at[axis] + (d + RING), RING)

    def roll(self, v, shift, axis):
        return pltpu.roll(v, shift, axis)

    def ready(self):
        pl.semaphore_wait(self.barrier, 3 * (RING - 1))

    def copy(self, src, dst, send_sem, recv_sem, axis, d):
        return pltpu.make_async_remote_copy(
            src_ref=src, dst_ref=dst, send_sem=send_sem, recv_sem=recv_sem,
            device_id={axis: self.peer(axis, d)}, device_id_type=pl.DeviceIdType.MESH)

    def shift_copy(self, name):
        axis, d, _, _ = SHIFTS[name]
        i = list(SHIFTS).index(name)
        return self.copy(
            self.refs["out" + name], self.refs["in" + name], self.refs["shift_sems"].at[0, i],
            self.refs["shift_sems"].at[1, i], axis, d)

    def shift_send(self, name, planes):
        ref = self.refs["out" + name]
        for i, v in enumerate(planes):
            ref[i] = v
        copy = self.shift_copy(name)
        copy.start()
        self.started.append(copy)

    def shift_recv(self, name):
        self.shift_copy(name).wait_recv()
        ref = self.refs["in" + name]
        return [ref[i] for i in range(SHIFTS[name][2])]

    def gather_send(self, name, v):
        axis, _ = GATHERS[name]
        i = list(GATHERS).index(name)
        me = self.at[axis]
        buf, src, sems = self.refs["in" + name], self.refs["out" + name], self.refs["gather_sems"]
        src[...] = v
        for d in (1, 7, 2, 6, 3, 5, 4):
            copy = self.copy(src, buf.at[me], sems.at[0, i, d], sems.at[1, i, me], axis, d)
            copy.start()
            self.started.append(copy)
        buf[me] = v

    def gather_recv(self, name):
        axis, _ = GATHERS[name]
        i = list(GATHERS).index(name)
        buf, src, sems = self.refs["in" + name], self.refs["out" + name], self.refs["gather_sems"]
        for d in range(1, RING):
            k = self.peer(axis, d)
            self.copy(src, buf.at[k], sems.at[0, i, d], sems.at[1, i, k], axis, d).wait_recv()
        return [buf[k] for k in range(RING)]

    def window(self, planes):
        ref = self.refs["planes3"]
        zero = jnp.zeros((16, LANES), jnp.float32)
        for z in (0, 1, 18, 19):
            ref[z] = zero
        for z, v in enumerate(planes):
            ref[z + 2] = v
        return [ref[2 * self.position[0] + s] for s in range(6)]

    def coarse_out(self, v):
        for z in range(4):
            self.refs["coarse"][z] = v[4 * z:4 * z + 4, :32]

    def fine_out(self, z, pressure, residual):
        self.refs["pressure"][z] = pressure
        self.refs["residual"][z] = residual

    def finish(self):
        for copy in self.started:
            copy.wait_send()


def scratch():
    shapes = {}
    for name, (_, _, count, rows) in SHIFTS.items():
        shapes["out" + name] = pltpu.VMEM((count, rows, LANES), jnp.float32)
        shapes["in" + name] = pltpu.VMEM((count, rows, LANES), jnp.float32)
    for name, (_, rows) in GATHERS.items():
        shapes["out" + name] = pltpu.VMEM((rows, LANES), jnp.float32)
        shapes["in" + name] = pltpu.VMEM((RING, rows, LANES), jnp.float32)
    shapes["planes3"] = pltpu.VMEM((20, 16, LANES), jnp.float32)
    shapes["shift_sems"] = pltpu.SemaphoreType.DMA((2, len(SHIFTS)))
    shapes["gather_sems"] = pltpu.SemaphoreType.DMA((2, len(GATHERS), RING))
    return shapes


def kernel(names, divergence, previous, pressure, residual, coarse, *buffers):
    refs = dict(zip(names, buffers), pressure=pressure, residual=residual, coarse=coarse)
    env = KernelEnv(refs)
    cycle(env, [previous[z] for z in range(16)], [divergence[z] for z in range(16)])
    env.finish()


def body(divergence, pressure_prev):
    shapes = scratch()
    block = jax.ShapeDtypeStruct((16, 16, 128), jnp.float32)
    vmem = pl.BlockSpec(memory_space=pltpu.VMEM)
    return pl.pallas_call(
        functools.partial(kernel, tuple(shapes)),
        out_shape=(block, block, jax.ShapeDtypeStruct((4, 4, 32), jnp.float32)),
        in_specs=[vmem, vmem],
        out_specs=(vmem, vmem, vmem),
        scratch_shapes=list(shapes.values()),
        compiler_params=pltpu.CompilerParams(
            collective_id=0, has_side_effects=True, vmem_limit_bytes=48 * 1024 * 1024),
        name="cycle",
    )(divergence, pressure_prev)


def solution(mesh):
    in_specs = (P("gz", "gx", "gy"), P("gz", "gx", "gy"))
    out_specs = (P("gz", "gx", "gy"), P("gz", "gx", "gy"), P())
    return jax.shard_map(body, mesh=mesh, in_specs=in_specs, out_specs=out_specs, check_vma=False)
```

```python
import functools

import jax
import jax.numpy as jnp
from jax import lax
from jax.experimental import pallas as pl
from jax.experimental.pallas import tpu as pltpu
from jax.sharding import PartitionSpec as P

FIRST = 1.0 / 7.5
RHO = 1.0 / (2.0 * (5.0 / 3.0) - 0.6)
CARRY = 0.6 * RHO
FRESH = 2.0 * RHO / (0.75 * 6.0)
ALPHA = FIRST * (1.0 + CARRY) + FRESH
BETA = FRESH * FIRST
OWN = ALPHA - 6.0 * BETA

LANES = 128
GROUPS2 = ((0, 1, 2), (3, 4), (5, 6, 7))
RING = 8

SHIFTS = {
    "fx+": ("gx", 1, 1, 16), "fx-": ("gx", -1, 1, 16),
    "fz+": ("gz", 1, 1, 16), "fz-": ("gz", -1, 1, 16),
    "fy+": ("gy", 1, 1, 16), "fy-": ("gy", -1, 1, 16),
    "x0+": ("gx", 1, 8, 8), "x0-": ("gx", -1, 8, 8),
    "x1+": ("gx", 1, 12, 8), "x1-": ("gx", -1, 12, 8),
    "x2+1": ("gx", 1, 3, 8), "x2-1": ("gx", -1, 3, 8),
    "x2+2": ("gx", 2, 3, 8), "x2-2": ("gx", -2, 3, 8),
    "z0+": ("gz", 1, 4, 24), "z0-": ("gz", -1, 4, 24),
    "z1+": ("gz", 1, 7, 24), "z1-": ("gz", -1, 7, 24),
    "z2+1": ("gz", 1, 3, 16), "z2-1": ("gz", -1, 3, 16),
    "z2+2": ("gz", 2, 1, 16), "z2-2": ("gz", -2, 1, 16),
    "y0+": ("gy", 1, 1, 24), "y0-": ("gy", -1, 1, 24),
    "y1+": ("gy", 1, 2, 24), "y1-": ("gy", -1, 2, 24),
    "y2+": ("gy", 1, 1, 16), "y2-": ("gy", -1, 1, 16),
    "y3+": ("gy", 1, 1, 16), "y3-": ("gy", -1, 1, 16),
}
GATHERS = {"gx3": ("gx", 8), "gz3": ("gz", 16), "gy4": ("gy", 8)}


def iota(shape, dim):
    return lax.broadcasted_iota(jnp.int32, shape, dim)


def number(cond):
    return jnp.where(cond, 1.0, 0.0).astype(jnp.float32)


def dot(a, b):
    return jnp.dot(a, b, precision=lax.Precision.HIGHEST, preferred_element_type=jnp.float32)


def select_matrix(shape, hit, value=1.0):
    return number(hit(iota(shape, 0), iota(shape, 1))) * value


def rows_of(stacked, rows):
    return [stacked[i * rows:(i + 1) * rows] for i in range(stacked.shape[0] // rows)]


def lanes_of(stacked):
    return [stacked[:, i * LANES:(i + 1) * LANES] for i in range(stacked.shape[1] // LANES)]


def right(planes, matrix):
    return rows_of(dot(jnp.concatenate(planes, axis=0), matrix), planes[0].shape[0])


def left(matrix, planes):
    return lanes_of(dot(matrix, jnp.concatenate(planes, axis=1)))


def total(terms):
    terms = [t for t in terms if t is not None]
    out = terms[0]
    for t in terms[1:]:
        out = out + t
    return out


class Field:
    def __init__(self, lo, hi, make):
        self.lo, self.hi, self.make, self.have = lo, hi, make, {}

    def __call__(self, z):
        if z < self.lo or z > self.hi:
            return None
        if z not in self.have:
            self.have[z] = self.make(z)
        return self.have[z]


def field_of(lo, planes):
    return Field(lo, lo + len(planes) - 1, lambda z: planes[z - lo])


class Math:
    def __init__(self, env):
        self.env = env
        self.iz, self.ix, self.iy = env.position

    def roll(self, v, shift, axis):
        shift = shift % v.shape[axis]
        return v if shift == 0 else self.env.roll(v, shift, axis)

    def place_rows(self, v, at, rows):
        pad = jnp.zeros((rows - v.shape[0],) + v.shape[1:], v.dtype)
        return self.roll(jnp.concatenate([v, pad], axis=0), at, 0)

    def take_rows(self, v, at, rows):
        return self.roll(v, -at, 0)[:rows]

    def mask(self, level, rows, row_off, lanes, own_y):
        nz, nx, ny = 16 >> level, 16 >> level, 128 >> level
        x = iota((rows, lanes), 0) - row_off + self.ix * nx
        lane = iota((rows, lanes), 1)
        y = jnp.where(lane < (own_y + lanes) // 2, lane, lane - lanes) + self.iy * ny
        flat = number((x >= 0) & (x < 128 >> level) & (y >= 0) & (y < 1024 >> level))

        def make(z):
            if 0 <= z < nz:
                return flat
            at = self.iz * nz + z
            return flat * number((at >= 0) & (at < 128 >> level))

        return Field(-16, 32, make)

    def beside(self, f, z):
        v = f(z)
        terms = [f(z - 1), f(z + 1)]
        if v is not None:
            terms += [self.roll(v, 1, 0), self.roll(v, -1, 0), self.roll(v, 1, 1), self.roll(v, -1, 1)]
        return total(terms)

    def correction(self, r, mask, lo, hi):
        def make(z):
            v = r(z)
            near = BETA * self.beside(r, z)
            return mask(z) * (near if v is None else OWN * v + near)
        return Field(lo, hi, make)

    def minus_op(self, b, x, mask, lo, hi):
        def make(z):
            out = self.beside(x, z)
            if x(z) is not None:
                out = out - 6.0 * x(z)
            if b(z) is not None:
                out = out + b(z)
            return mask(z) * out
        return Field(lo, hi, make)

    def slots(self, rows, start, width):
        lane = (iota((rows, LANES), 1) - start) & (LANES - 1)
        return number(lane < width)

    def pack(self, planes, start, width=8):
        rows, per = planes[0].shape[0], LANES // width
        tiles = []
        for g in range(0, len(planes), per):
            tiles.append(total([
                self.slots(rows, width * w, width) * self.roll(plane, width * w - start, 1)
                for w, plane in enumerate(planes[g:g + per])
            ]))
        return tiles

    def unpack(self, tiles, count, start, width=8):
        keep, per = self.slots(tiles[0].shape[0], start, width), LANES // width
        return [keep * self.roll(tiles[i // per], start - width * (i % per), 1) for i in range(count)]


def cycle(env, x_own, b_own):
    m = Math(env)
    iz, ix, iy = env.position
    zeros = lambda *s: jnp.zeros(s, jnp.float32)

    mask0 = m.mask(0, 24, 4, 256, 128)
    put0 = lambda v: jnp.concatenate([m.place_rows(v, 4, 24), zeros(24, LANES)], axis=1)
    xc = Field(0, 15, lambda z: put0(x_own[z]))
    bc = Field(0, 15, lambda z: put0(b_own[z]))
    r0 = m.minus_op(bc, xc, mask0, -1, 16)
    u0 = m.correction(r0, mask0, -2, 17)
    p0 = m.minus_op(r0, u0, mask0, -3, 18)
    coarse = [total([p0(2 * z), p0(2 * z + 1)]) for z in range(-2, 10)]
    coarse = right(coarse, select_matrix((256, 128), lambda a, c: (a >> 1) == c, 0.5))
    coarse = left(select_matrix((16, 24), lambda a, c: (c >> 1) + 2 == a), coarse)
    mask1c = m.mask(1, 16, 4, 128, 64)
    b1c = field_of(-2, [mask1c(z) * v for z, v in zip(range(-2, 10), coarse)])

    u1 = m.correction(b1c, mask1c, -3, 10)
    p1 = m.minus_op(b1c, u1, mask1c, -4, 11)
    coarse = [total([p1(2 * z), p1(2 * z + 1)]) for z in range(-2, 6)]
    half = select_matrix((128, 128), lambda a, c: (a >> 1) + jnp.where(a >= 96, 64, 0) == c, 0.5)
    coarse = right(coarse, half)
    halve_rows = select_matrix((8, 16), lambda a, c: (c >> 1) == a)
    coarse = left(halve_rows, coarse)
    mask2e = m.mask(2, 8, 2, 128, 32)
    b2c = [mask2e(z) * v for z, v in zip(range(-2, 6), coarse)]

    mask2c = m.mask(2, 16, 4, 128, 32)
    b2p = field_of(-2, [m.place_rows(v, 2, 16) for v in b2c])
    u2 = m.correction(b2p, mask2c, -3, 6)
    p2 = m.minus_op(b2p, u2, mask2c, -4, 7)
    coarse = [total([p2(2 * z), p2(2 * z + 1)]) for z in range(-2, 4)]
    half = select_matrix((128, 128), lambda a, c: (jnp.where(a < 80, a, a - 128) >> 1) + 2 == c, 0.5)
    coarse = left(halve_rows, right(coarse, half))
    b3c = total([m.roll(v, 20 * s, 1) for s, v in enumerate(coarse)])

    env.ready()
    env.gather_send("gx3", b3c)
    env.shift_send("fx+", [env.row(x_own, 15)])
    env.shift_send("fx-", [env.row(x_own, 0)])
    env.shift_send("fz+", [x_own[15]])
    env.shift_send("fz-", [x_own[0]])
    lane16 = iota((16, LANES), 1)
    env.shift_send("fy+", m.pack(x_own, 127, 1))
    env.shift_send("fy-", m.pack(x_own, 0, 1))
    packed2 = [total([m.roll(b2c[i], 40 * w + 2, 1) for w, i in enumerate(g)]) for g in GROUPS2]
    for d in (1, -1, 2, -2):
        env.shift_send("x2%+d" % d, packed2)
    env.shift_send("x1+", [m.take_rows(b1c(z), 7, 8) for z in range(-2, 10)])
    env.shift_send("x1-", [m.take_rows(b1c(z), 2, 8) for z in range(-2, 10)])

    row_a, lane_a = iota((16, LANES), 0), iota((16, LANES), 1)
    inside = lambda at: (number(at > 0), number(at < RING - 1))
    (z_lo, z_hi), (x_lo, x_hi), (y_lo, y_hi) = inside(iz), inside(ix), inside(iy)
    row_first, row_last = x_lo * number(row_a == 0), x_hi * number(row_a == 15)
    row_later, row_sooner = number(row_a > 0), number(row_a < 15)
    y_first, y_last = y_lo * number(lane_a == 0), y_hi * number(lane_a == 127)
    y_later, y_sooner = number(lane_a > 0), number(lane_a < 127)
    fx_lo, fx_hi = env.shift_recv("fx+")[0], env.shift_recv("fx-")[0]
    fz_lo, fz_hi = z_lo * env.shift_recv("fz+")[0], z_hi * env.shift_recv("fz-")[0]
    fy_lo, fy_hi = env.shift_recv("fy+")[0], env.shift_recv("fy-")[0]
    r_own = []
    for z in range(16):
        v = x_own[z]
        near = (x_own[z - 1] if z else fz_lo) + (x_own[z + 1] if z < 15 else fz_hi)
        near = near + row_later * m.roll(v, 1, 0) + row_first * fx_lo[z:z + 1]
        near = near + row_sooner * m.roll(v, -1, 0) + row_last * fx_hi[z:z + 1]
        near = near + y_later * m.roll(v, 1, 1) + y_first * m.roll(fy_lo, -z, 1)
        near = near + y_sooner * m.roll(v, -1, 1) + y_last * m.roll(fy_hi, 127 - z, 1)
        r_own.append(b_own[z] - 6.0 * v + near)
    row8 = iota((8, LANES), 0)
    is_low = row8 < 4
    two = lambda a, b: jnp.where(is_low, a, b)
    half = lambda v: m.roll(v, 4, 0)
    env.shift_send("x0+", [two(half(r_own[2 * i][8:]), r_own[2 * i + 1][8:]) for i in range(8)])
    env.shift_send("x0-", [two(r_own[2 * i][:8], half(r_own[2 * i + 1][:8])) for i in range(8)])

    parts = env.gather_recv("gx3")
    wide = total([m.place_rows(v, 2 * k, 24) for k, v in enumerate(parts)])
    b3x = m.take_rows(wide, 2, 16)

    env.gather_send("gz3", b3x)

    before, after = env.shift_recv("x0+"), env.shift_recv("x0-")
    r0x = []
    for z in range(16):
        low, high = half(r_own[z][:8]), half(r_own[z][8:])
        lo, hi = before[z // 2], after[z // 2]
        if z % 2:
            lo = half(lo)
        else:
            hi = half(hi)
        r0x.append(jnp.concatenate([two(lo, low), two(low, high), two(high, hi)], axis=0))
    env.shift_send("z0+", r0x[12:])
    env.shift_send("z0-", r0x[:4])

    got = {d: env.shift_recv("x2%+d" % d) for d in (1, -1, 2, -2)}
    low, high = number(row8 < 4), number(row8 >= 4)
    b2x = []
    for i in range(3):
        lo = got[1][i] + low * half(got[2][i])
        hi = got[-1][i] + high * half(got[-2][i])
        b2x.append(jnp.concatenate([lo, hi], axis=0) + m.place_rows(packed2[i], 4, 16))
    env.shift_send("z2+1", b2x)
    env.shift_send("z2-1", b2x)
    env.shift_send("z2+2", b2x[2:])
    env.shift_send("z2-2", b2x[:1])

    before, after = env.shift_recv("x1+"), env.shift_recv("x1-")
    b1x = [
        m.place_rows(b1c(i - 2), 4, 24) + m.place_rows(before[i], 3, 24) + m.place_rows(after[i], 14, 24)
        for i in range(12)
    ]
    env.shift_send("z1+", b1x[5:])
    env.shift_send("z1-", b1x[:7])

    r0w = env.shift_recv("z0+") + r0x + env.shift_recv("z0-")
    env.shift_send("y0+", m.pack(r0w, 124, 4))
    env.shift_send("y0-", m.pack(r0w, 0, 4))

    parts = env.gather_recv("gz3")
    lane = iota((16, LANES), 1)
    tiles = []
    for q in range(4):
        tile = None
        for w in range(4):
            z = 4 * q + w
            here = []
            for k in range(RING):
                s = z - 2 * k + 2
                if 0 <= s < 6:
                    here.append(m.roll(parts[k], 32 * w + 6 - 20 * s, 1))
            at = lane - (32 * w + 6)
            part = number((at >= 0) & (at < 20)) * total(here)
            tile = part if tile is None else tile + part
        tiles.append(tile)
    row16, lane512 = iota((16, 512), 0), iota((16, 512), 1)
    slot = lane512 & 31
    y3 = slot - 8 + 16 * iy
    mask3 = number((y3 >= 0) & (y3 < 128))
    not_first, not_last = number(row16 > 0), number(row16 < 15)
    not_bottom, not_top = number(lane512 >= 32), number(lane512 < 480)

    def beside3(v):
        out = not_first * m.roll(v, 1, 0) + not_last * m.roll(v, -1, 0)
        out = out + not_bottom * m.roll(v, 32, 1) + not_top * m.roll(v, -32, 1)
        return out + m.roll(v, 1, 1) + m.roll(v, -1, 1)

    correction3 = lambda r: mask3 * (OWN * r + BETA * beside3(r))
    minus_op3 = lambda b, x: mask3 * (b - 6.0 * x + beside3(x))

    b3s = mask3 * jnp.concatenate(tiles, axis=1)
    p3 = minus_op3(b3s, correction3(b3s))
    gather_lanes = select_matrix((512, 128), lambda a, c: 16 * (a >> 6) + ((a & 31) >> 1) == c, 0.5)
    b4c = dot(halve_rows, dot(p3, gather_lanes))

    env.gather_send("gy4", b4c)
    octet = (lane >> 3) & 3
    squeeze = lambda at: total([
        number(octet == q) * m.roll(v, 8 * q - at, 1) for q, v in enumerate(lanes_of(b3s))
    ])
    env.shift_send("y3+", [squeeze(19)])
    env.shift_send("y3-", [squeeze(6)])

    got = {d: env.shift_recv("z2%+d" % d) for d in (1, -1, 2, -2)}
    keep = m.slots(16, 126, 40)

    def plane2(groups, i):
        g = [i in group for group in GROUPS2].index(True)
        return m.roll(groups[g], -(40 * GROUPS2[g].index(i) + 2), 1)

    b2w = []
    for z in range(-5, 9):
        here = []
        if -2 <= z <= 5:
            here.append(plane2(b2x, z + 2))
        if z <= 1:
            here.append(plane2(got[1], z + 6))
        if z >= 2:
            here.append(plane2(got[-1], z - 2))
        if z <= -3:
            here.append(plane2([None, None] + got[2], z + 10))
        if z >= 6:
            here.append(plane2(got[-2], z - 6))
        b2w.append(keep * total(here))
    env.shift_send("y2+", m.pack(b2w, 27))
    env.shift_send("y2-", m.pack(b2w, 126))

    before, after = env.shift_recv("z1+"), env.shift_recv("z1-")
    b1w = []
    for z in range(-5, 13):
        here = []
        if -2 <= z <= 9:
            here.append(b1x[z + 2])
        if z <= 1:
            here.append(before[z + 5])
        if z >= 6:
            here.append(after[z - 6])
        b1w.append(total(here))
    env.shift_send("y1+", m.pack(b1w, 59))
    env.shift_send("y1-", m.pack(b1w, 126))

    before, after = env.shift_recv("y3+")[0], env.shift_recv("y3-")[0]
    slot16 = lane16 & 31
    low_slot, high_slot = number((slot16 >= 3) & (slot16 < 11)), number((slot16 >= 22) & (slot16 < 30))
    b3w = mask3 * (b3s + jnp.concatenate([
        low_slot * m.roll(before, 3 - 8 * q, 1) + high_slot * m.roll(after, 22 - 8 * q, 1) for q in range(4)
    ], axis=1))
    u3 = correction3(b3w)
    p3 = minus_op3(b3w, u3)

    mask0 = m.mask(0, 24, 4, 256, 128)
    low = m.unpack(env.shift_recv("y0+"), 24, 124, 4)
    high = m.unpack(env.shift_recv("y0-"), 24, 0, 4)
    r0 = field_of(-4, [
        mask0(i - 4) * jnp.concatenate([v, low[i] + high[i]], axis=1) for i, v in enumerate(r0w)
    ])
    u0 = m.correction(r0, mask0, -3, 18)
    p0 = m.minus_op(r0, u0, mask0, -2, 17)

    parts = env.gather_recv("gy4")
    row, lane = iota((8, LANES), 0), iota((8, LANES), 1)
    keep = []
    for j in range(RING):
        at = lane - (8 * j - 4)
        keep.append(number((at >= 0) & (at < 16) & (lane < 64)))
    b4 = field_of(0, [
        total([keep[j] * m.roll(parts[j], 8 * j - 4 - 16 * z, 1) for j in range(RING)]) for z in range(8)
    ])
    mask4 = number(lane < 64)
    first8, last8 = number(row > 0), number(row < 7)

    def beside4(f, z):
        v = f(z)
        return total([
            f(z - 1), f(z + 1), first8 * m.roll(v, 1, 0), last8 * m.roll(v, -1, 0), m.roll(v, 1, 1), m.roll(v, -1, 1)
        ])

    def correction4(r):
        return Field(0, 7, lambda z: mask4 * (OWN * r(z) + BETA * beside4(r, z)))

    def minus_op4(b, x):
        return Field(0, 7, lambda z: mask4 * (b(z) - 6.0 * x(z) + beside4(x, z)))

    u4 = correction4(b4)
    p4 = minus_op4(b4, u4)
    half = select_matrix((128, 128), lambda a, c: ((a >> 1) == c) & (a < 64), 0.5)
    coarse = jnp.concatenate([p4(2 * z) + p4(2 * z + 1) for z in range(4)], axis=0)
    b5 = dot(select_matrix((16, 32), lambda a, c: (c >> 3) * 4 + ((c & 7) >> 1) == a), dot(coarse, half))

    row, lane = iota((16, LANES), 0), iota((16, LANES), 1)
    mask5 = number(lane < 32)
    first5, last5 = number((row & 3) > 0), number((row & 3) < 3)
    bottom5, top5 = number(row >= 4), number(row < 12)

    def beside5(v):
        out = first5 * m.roll(v, 1, 0) + last5 * m.roll(v, -1, 0)
        out = out + bottom5 * m.roll(v, 4, 0) + top5 * m.roll(v, -4, 0)
        return out + m.roll(v, 1, 1) + m.roll(v, -1, 1)

    u5 = mask5 * (OWN * b5 + BETA * beside5(b5))
    p5 = mask5 * (b5 - 6.0 * u5 + beside5(u5))
    e5 = u5 + mask5 * (OWN * p5 + BETA * beside5(p5))
    env.coarse_out(e5)

    double = select_matrix((128, 128), lambda a, c: (a == (c >> 1)) & (c < 64))
    wide = dot(select_matrix((32, 16), lambda a, c: (a >> 3) * 4 + ((a & 7) >> 1) == c), dot(e5, double))
    c4 = rows_of(wide, 8)
    c4 = field_of(0, [c4[z // 2] for z in range(8)])
    q4 = minus_op4(p4, c4)
    v4 = correction4(q4)
    e4 = [u4(z) + c4(z) + v4(z) for z in range(8)]

    own_y = select_matrix((128, 128), lambda a, c: (a == 8 * iy + (((c & 31) - 8) >> 1)) & (c < 64))
    planes = right(e4, own_y)
    wide = jnp.concatenate([planes[2 * k] + m.roll(planes[2 * k + 1], 64, 1) for k in range(4)], axis=1)
    c3 = mask3 * dot(select_matrix((16, 8), lambda a, c: (a >> 1) == c), wide)
    e3 = u3 + c3 + correction3(minus_op3(p3, c3))

    spread = select_matrix((16, 16), lambda a, c: 2 * ix + ((a - 6) >> 1) == c)
    tiles = lanes_of(dot(spread, e3))
    near = env.window([m.roll(tiles[z // 4], -32 * (z % 4), 1) for z in range(16)])
    y_of = lambda c: jnp.where(c < 80, c, c - 128)
    own_y = select_matrix(
        (128, 128), lambda a, c: (a - 8 == (y_of(c) >> 1)) & (a < 32) & (y_of(c) < 36) & (y_of(c) >= -4))
    near = right(near, own_y)
    c2 = field_of(-4, [near[(z >> 1) + 2] for z in range(-4, 8)])

    def window(level, planes, tag, rows, row_off, lo, own_y, at_low, at_high):
        mask = m.mask(level, rows, row_off, LANES, own_y)
        before = m.unpack(env.shift_recv(tag + "+"), len(planes), at_low)
        after = m.unpack(env.shift_recv(tag + "-"), len(planes), at_high)
        return mask, field_of(lo, [
            mask(lo + i) * (v + before[i] + after[i]) for i, v in enumerate(planes)
        ])

    mask2, b2 = window(2, b2w, "y2", 16, 6, -5, 32, 123, 30)
    u2 = m.correction(b2, mask2, -4, 7)
    p2 = m.minus_op(b2, u2, mask2, -3, 6)
    v2 = m.correction(m.minus_op(p2, c2, mask2, -3, 6), mask2, -2, 5)
    e2 = [u2(z) + mask2(z) * c2(z) + v2(z) for z in range(-2, 6)]

    y_fine = lambda c: jnp.where(c < 96, c, c - 128)
    own_y = select_matrix((128, 128), lambda a, c: y_of(a) == (y_fine(c) >> 1))
    coarse = left(select_matrix((24, 16), lambda a, c: (a >> 1) + 2 == c), e2)
    coarse = right(coarse, own_y)
    c1 = field_of(-4, [coarse[(z >> 1) + 2] for z in range(-4, 12)])
    mask1, b1 = window(1, b1w, "y1", 24, 8, -5, 64, 123, 62)
    u1 = m.correction(b1, mask1, -4, 11)
    p1 = m.minus_op(b1, u1, mask1, -3, 10)
    v1 = m.correction(m.minus_op(p1, c1, mask1, -3, 10), mask1, -2, 9)
    e1 = [u1(z) + mask1(z) * c1(z) + v1(z) for z in range(-2, 10)]

    coarse = left(select_matrix((24, 24), lambda a, c: ((a - 4) >> 1) + 8 == c), e1)
    coarse = right(coarse, select_matrix((128, 256), lambda a, c: a == (c >> 1)))
    c0 = field_of(-4, [coarse[(z >> 1) + 2] for z in range(-4, 20)])
    q0 = m.minus_op(p0, c0, mask0, -2, 17)
    v0 = m.correction(q0, mask0, -1, 16)
    left_over = m.minus_op(q0, v0, mask0, 0, 15)
    inner = lambda v: m.take_rows(v[:, :LANES], 4, 16)
    for z in range(16):
        env.fine_out(z, x_own[z] + inner(u0(z) + c0(z) + v0(z)), inner(left_over(z)))


class KernelEnv:
    def __init__(self, refs):
        self.refs = refs
        self.position = tuple(lax.axis_index(a) for a in ("gz", "gx", "gy"))
        self.at = dict(zip(("gz", "gx", "gy"), self.position))
        self.started = []
        self.barrier = pltpu.get_barrier_semaphore()
        for axis in ("gx", "gz", "gy"):
            for d in range(1, RING):
                pl.semaphore_signal(
                    self.barrier, inc=1, device_id={axis: self.peer(axis, d)}, device_id_type=pl.DeviceIdType.MESH)

    def peer(self, axis, d):
        return lax.rem(self.at[axis] + (d + RING), RING)

    def roll(self, v, shift, axis):
        return pltpu.roll(v, shift, axis)

    def row(self, planes, x):
        return self.refs["previous"][pl.ds(x, 16, stride=16), :]

    def ready(self):
        pl.semaphore_wait(self.barrier, 3 * (RING - 1))

    def copy(self, src, dst, send_sem, recv_sem, axis, d):
        return pltpu.make_async_remote_copy(
            src_ref=src, dst_ref=dst, send_sem=send_sem, recv_sem=recv_sem,
            device_id={axis: self.peer(axis, d)}, device_id_type=pl.DeviceIdType.MESH)

    def shift_copy(self, name):
        axis, d, _, _ = SHIFTS[name]
        i = list(SHIFTS).index(name)
        return self.copy(
            self.refs["out" + name], self.refs["in" + name], self.refs["shift_sems"].at[0, i],
            self.refs["shift_sems"].at[1, i], axis, d)

    def shift_send(self, name, planes):
        ref = self.refs["out" + name]
        for i, v in enumerate(planes):
            ref[i] = v
        copy = self.shift_copy(name)
        copy.start()
        self.started.append(copy)

    def shift_recv(self, name):
        self.shift_copy(name).wait_recv()
        ref = self.refs["in" + name]
        return [ref[i] for i in range(SHIFTS[name][2])]

    def gather_send(self, name, v):
        axis, _ = GATHERS[name]
        i = list(GATHERS).index(name)
        me = self.at[axis]
        buf, src, sems = self.refs["in" + name], self.refs["out" + name], self.refs["gather_sems"]
        src[...] = v
        for d in (4, 3, 5, 2, 6, 1, 7):
            copy = self.copy(src, buf.at[me], sems.at[0, i, d], sems.at[1, i, me], axis, d)
            copy.start()
            self.started.append(copy)
        buf[me] = v

    def gather_recv(self, name):
        axis, _ = GATHERS[name]
        i = list(GATHERS).index(name)
        buf, src, sems = self.refs["in" + name], self.refs["out" + name], self.refs["gather_sems"]
        for d in range(1, RING):
            k = self.peer(axis, d)
            self.copy(src, buf.at[k], sems.at[0, i, d], sems.at[1, i, k], axis, d).wait_recv()
        return [buf[k] for k in range(RING)]

    def window(self, planes):
        ref = self.refs["planes3"]
        zero = jnp.zeros((16, LANES), jnp.float32)
        for z in (0, 1, 18, 19):
            ref[z] = zero
        for z, v in enumerate(planes):
            ref[z + 2] = v
        return [ref[2 * self.position[0] + s] for s in range(6)]

    def coarse_out(self, v):
        for z in range(4):
            self.refs["coarse"][z] = v[4 * z:4 * z + 4, :32]

    def fine_out(self, z, pressure, residual):
        self.refs["pressure"][z] = pressure
        self.refs["residual"][z] = residual

    def finish(self):
        for copy in self.started:
            copy.wait_send()


def scratch():
    shapes = {}
    for name, (_, _, count, rows) in SHIFTS.items():
        shapes["out" + name] = pltpu.VMEM((count, rows, LANES), jnp.float32)
        shapes["in" + name] = pltpu.VMEM((count, rows, LANES), jnp.float32)
    for name, (_, rows) in GATHERS.items():
        shapes["out" + name] = pltpu.VMEM((rows, LANES), jnp.float32)
        shapes["in" + name] = pltpu.VMEM((RING, rows, LANES), jnp.float32)
    shapes["previous"] = pltpu.VMEM((256, LANES), jnp.float32)
    shapes["divergence"] = pltpu.VMEM((256, LANES), jnp.float32)
    shapes["load_sems"] = pltpu.SemaphoreType.DMA((2,))
    shapes["planes3"] = pltpu.VMEM((20, 16, LANES), jnp.float32)
    shapes["shift_sems"] = pltpu.SemaphoreType.DMA((2, len(SHIFTS)))
    shapes["gather_sems"] = pltpu.SemaphoreType.DMA((2, len(GATHERS), RING))
    return shapes


def kernel(names, divergence, previous, pressure, residual, coarse, *buffers):
    refs = dict(zip(names, buffers), pressure=pressure, residual=residual, coarse=coarse)
    loads = [
        pltpu.make_async_copy(previous, refs["previous"], refs["load_sems"].at[0]),
        pltpu.make_async_copy(divergence, refs["divergence"], refs["load_sems"].at[1]),
    ]
    for load in loads:
        load.start()
    env = KernelEnv(refs)
    for load in loads:
        load.wait()
    planes = lambda name: [refs[name][16 * z:16 * z + 16] for z in range(16)]
    cycle(env, planes("previous"), planes("divergence"))
    env.finish()


def store_kernel(*refs):
    values, outs, sems = refs[:3], refs[3:6], refs[6]
    copies = [pltpu.make_async_copy(v, o, sems.at[i]) for i, (v, o) in enumerate(zip(values, outs))]
    for copy in copies:
        copy.start()
    for copy in copies:
        copy.wait()


def body(divergence, pressure_prev):
    shapes = scratch()
    block = jax.ShapeDtypeStruct((16, 16, 128), jnp.float32)
    outs = (block, block, jax.ShapeDtypeStruct((4, 4, 32), jnp.float32))
    vmem, hbm = pl.BlockSpec(memory_space=pltpu.VMEM), pl.BlockSpec(memory_space=pltpu.HBM)
    results = pl.pallas_call(
        functools.partial(kernel, tuple(shapes)),
        out_shape=outs,
        in_specs=[hbm, hbm],
        out_specs=(vmem, vmem, vmem),
        scratch_shapes=list(shapes.values()),
        compiler_params=pltpu.CompilerParams(
            collective_id=0, has_side_effects=True, vmem_limit_bytes=48 * 1024 * 1024),
        name="cycle",
    )(*(pltpu.with_memory_space_constraint(v.reshape(256, 128), pltpu.HBM) for v in (divergence, pressure_prev)))
    return pl.pallas_call(
        store_kernel,
        out_shape=outs,
        in_specs=[vmem, vmem, vmem],
        out_specs=(hbm, hbm, hbm),
        scratch_shapes=[pltpu.SemaphoreType.DMA((3,))],
        compiler_params=pltpu.CompilerParams(vmem_limit_bytes=1024 * 1024),
        name="store",
    )(*results)


def solution(mesh):
    in_specs = (P("gz", "gx", "gy"), P("gz", "gx", "gy"))
    out_specs = (P("gz", "gx", "gy"), P("gz", "gx", "gy"), P())
    return jax.shard_map(body, mesh=mesh, in_specs=in_specs, out_specs=out_specs, check_vma=False)
```

```python
import functools

import jax
import jax.numpy as jnp
from jax import lax
from jax.experimental import pallas as pl
from jax.experimental.pallas import tpu as pltpu
from jax.sharding import PartitionSpec as P

FIRST = 1.0 / 7.5
RHO = 1.0 / (2.0 * (5.0 / 3.0) - 0.6)
CARRY = 0.6 * RHO
FRESH = 2.0 * RHO / (0.75 * 6.0)
ALPHA = FIRST * (1.0 + CARRY) + FRESH
BETA = FRESH * FIRST
OWN = ALPHA - 6.0 * BETA

LANES = 128
GROUPS2 = ((0, 1, 2), (3, 4), (5, 6, 7))
RING = 8

SHIFTS = {
    "fx+": ("gx", 1, 1, 16), "fx-": ("gx", -1, 1, 16),
    "fz+": ("gz", 1, 1, 16), "fz-": ("gz", -1, 1, 16),
    "fy+": ("gy", 1, 1, 16), "fy-": ("gy", -1, 1, 16),
    "x0+": ("gx", 1, 8, 8), "x0-": ("gx", -1, 8, 8),
    "x1+": ("gx", 1, 12, 8), "x1-": ("gx", -1, 12, 8),
    "x2+1": ("gx", 1, 3, 8), "x2-1": ("gx", -1, 3, 8),
    "x2+2": ("gx", 2, 3, 8), "x2-2": ("gx", -2, 3, 8),
    "z0+": ("gz", 1, 4, 24), "z0-": ("gz", -1, 4, 24),
    "z1+": ("gz", 1, 7, 24), "z1-": ("gz", -1, 7, 24),
    "z2+1": ("gz", 1, 3, 16), "z2-1": ("gz", -1, 3, 16),
    "z2+2": ("gz", 2, 1, 16), "z2-2": ("gz", -2, 1, 16),
    "y0+": ("gy", 1, 1, 24), "y0-": ("gy", -1, 1, 24),
    "y1+": ("gy", 1, 2, 24), "y1-": ("gy", -1, 2, 24),
    "y2+": ("gy", 1, 1, 16), "y2-": ("gy", -1, 1, 16),
    "y3+": ("gy", 1, 1, 16), "y3-": ("gy", -1, 1, 16),
}
GATHERS = {"gx3": ("gx", 8), "gz3": ("gz", 16), "gy4": ("gy", 8)}


KEPT = {
    "s0": (16, 16, 128), "p0": (20, 24, 256), "u1": (12, 24, 128), "p1": (14, 24, 128),
    "u2": (8, 16, 128), "p2": (10, 16, 128), "u3": (1, 16, 512), "p3": (1, 16, 512),
}
MATRICES = {
    "lanes3": (512, 128), "lanes4": (128, 128), "up5": (128, 128), "up4": (128, 128), "up3": (128, 128),
    "up2": (128, 128), "up1": (128, 256), "next3": (128, 128), "next2": (128, 128), "next1": (128, 256),
}


def iota(shape, dim):
    return lax.broadcasted_iota(jnp.int32, shape, dim)


def number(cond):
    return jnp.where(cond, 1.0, 0.0).astype(jnp.float32)


def parts_of(v):
    high = v.astype(jnp.bfloat16)
    return high, (v - high.astype(jnp.float32)).astype(jnp.bfloat16)


def product(a, b):
    return jnp.dot(a, b, preferred_element_type=jnp.float32)


def times(v, matrix):
    high, low = parts_of(v)
    if v.shape[1] == LANES:
        return product(jnp.concatenate([high, low], axis=1), jnp.concatenate([matrix, matrix], axis=0))
    return product(high, matrix) + product(low, matrix)


def onto(matrix, v):
    high, low = parts_of(v)
    return product(matrix, high) + product(matrix, low)


def select_matrix(shape, hit, value=1.0):
    return jnp.where(hit(iota(shape, 0), iota(shape, 1)), value, 0.0).astype(jnp.bfloat16)


def rows_of(stacked, rows):
    return [stacked[i * rows:(i + 1) * rows] for i in range(stacked.shape[0] // rows)]


def lanes_of(stacked):
    return [stacked[:, i * LANES:(i + 1) * LANES] for i in range(stacked.shape[1] // LANES)]


def right(planes, matrix):
    return rows_of(times(jnp.concatenate(planes, axis=0), matrix), planes[0].shape[0])


def left(matrix, planes):
    return lanes_of(onto(matrix, jnp.concatenate(planes, axis=1)))


def widen(own, beside, rows, up, following):
    (own_high, own_low), (beside_high, beside_low) = parts_of(own), parts_of(beside)
    join = lambda a, b: jnp.concatenate([a, b], axis=1)
    inner = product(join(own_high, own_low), jnp.concatenate([up, up], axis=0))
    both = jnp.concatenate([up, following], axis=0)
    outer = product(join(beside_high, own_high), both) + product(join(beside_low, own_low), both)
    return rows_of(inner, rows), rows_of(outer, rows)


def halves(planes):
    rows = planes[0].shape[0] // 2
    return jnp.concatenate([v[:rows] for v in planes], axis=0), jnp.concatenate([v[rows:] for v in planes], axis=0), rows


def total(terms):
    terms = [t for t in terms if t is not None]
    out = terms[0]
    for t in terms[1:]:
        out = out + t
    return out


class Field:
    def __init__(self, lo, hi, make):
        self.lo, self.hi, self.make, self.have = lo, hi, make, {}

    def __call__(self, z):
        if z < self.lo or z > self.hi:
            return None
        if z not in self.have:
            self.have[z] = self.make(z)
        return self.have[z]


def field_of(lo, planes):
    return Field(lo, lo + len(planes) - 1, lambda z: planes[z - lo])


class Math:
    def __init__(self, env):
        self.env = env
        self.iz, self.ix, self.iy = env.position

    def roll(self, v, shift, axis):
        shift = shift % v.shape[axis]
        return v if shift == 0 else self.env.roll(v, shift, axis)

    def place_rows(self, v, at, rows):
        pad = jnp.zeros((rows - v.shape[0],) + v.shape[1:], v.dtype)
        return self.roll(jnp.concatenate([v, pad], axis=0), at, 0)

    def take_rows(self, v, at, rows):
        return self.roll(v, -at, 0)[:rows]

    def mask(self, level, rows, row_off, lanes, own_y):
        nz, nx, ny = 16 >> level, 16 >> level, 128 >> level
        x = iota((rows, lanes), 0) - row_off + self.ix * nx
        lane = iota((rows, lanes), 1)
        y = jnp.where(lane < (own_y + lanes) // 2, lane, lane - lanes) + self.iy * ny
        flat = number((x >= 0) & (x < 128 >> level) & (y >= 0) & (y < 1024 >> level))

        def make(z):
            if 0 <= z < nz:
                return flat
            at = self.iz * nz + z
            return flat * number((at >= 0) & (at < 128 >> level))

        return Field(-16, 32, make)

    def beside(self, f, z):
        v = f(z)
        terms = [f(z - 1), f(z + 1)]
        if v is not None:
            terms += [self.roll(v, 1, 0), self.roll(v, -1, 0), self.roll(v, 1, 1), self.roll(v, -1, 1)]
        return total(terms)

    def correction(self, r, mask, lo, hi):
        def make(z):
            v = r(z)
            near = BETA * self.beside(r, z)
            return mask(z) * (near if v is None else OWN * v + near)
        return Field(lo, hi, make)

    def minus_op(self, b, x, mask, lo, hi):
        def make(z):
            out = self.beside(x, z)
            if x(z) is not None:
                out = out - 6.0 * x(z)
            if b(z) is not None:
                out = out + b(z)
            return out if mask is None else mask(z) * out
        return Field(lo, hi, make)

    def minus_op_of_coarse(self, b, inner, outer, lo_coarse, mask, lo, hi):
        def make(z):
            at = (z >> 1) - lo_coarse
            return mask(z) * (b(z) + outer[at] + inner[at + 2 * (z & 1) - 1] - 3.0 * inner[at])
        return Field(lo, hi, make)

    def slots(self, rows, start, width):
        lane = (iota((rows, LANES), 1) - start) & (LANES - 1)
        return number(lane < width)

    def pack(self, planes, start, width=8):
        rows, per = planes[0].shape[0], LANES // width
        tiles = []
        for g in range(0, len(planes), per):
            tiles.append(total([
                self.slots(rows, width * w, width) * self.roll(plane, width * w - start, 1)
                for w, plane in enumerate(planes[g:g + per])
            ]))
        return tiles

    def unpack(self, tiles, count, start, width=8):
        keep, per = self.slots(tiles[0].shape[0], start, width), LANES // width
        return [keep * self.roll(tiles[i // per], start - width * (i % per), 1) for i in range(count)]


class Selections:
    def __init__(self, ix, iy):
        self.lanes0 = select_matrix((256, 128), lambda a, c: (a >> 1) == c, 0.5)
        self.rows0 = select_matrix((16, 24), lambda a, c: (c >> 1) + 2 == a)
        self.lanes1 = select_matrix((128, 128), lambda a, c: (a >> 1) + jnp.where(a >= 96, 64, 0) == c, 0.5)
        self.halve_rows = select_matrix((8, 16), lambda a, c: (c >> 1) == a)
        self.lanes2 = select_matrix((128, 128), lambda a, c: (jnp.where(a < 80, a, a - 128) >> 1) + 2 == c, 0.5)
        self.ix, self.iy = ix, iy

    def rest(self, env):
        ix, iy = self.ix, self.iy
        y_of = lambda c: jnp.where(c < 80, c, c - 128)
        y_fine = lambda c: jnp.where(c < 96, c, c - 128)
        side = lambda c: 2 * (c & 1) - 1

        def up_rows(rows, depth, coarse):
            fine = lambda a: jnp.where(a >= rows, a - rows, a)
            return select_matrix((2 * rows, depth), lambda a, c: (
                coarse(fine(a)) + jnp.where(a >= rows, side(fine(a)), 0) == c))

        hits = {
            "lanes3": lambda a, c: 16 * (a >> 6) + ((a & 31) >> 1) == c,
            "lanes4": lambda a, c: ((a >> 1) == c) & (a < 64),
            "up5": lambda a, c: (a == (c >> 1)) & (c < 64),
            "up4": lambda a, c: (a == 8 * iy + (((c & 31) - 8) >> 1)) & (c < 64),
            "up3": lambda a, c: (a - 8 == (y_of(c) >> 1)) & (a < 32) & (y_of(c) < 36) & (y_of(c) >= -4),
            "up2": lambda a, c: y_of(a) == (y_fine(c) >> 1),
            "up1": lambda a, c: a == (c >> 1),
            "next3": lambda a, c: (
                (a - 8 == (y_of(c) >> 1) + side(c)) & (a < 32) & (y_of(c) < 36) & (y_of(c) >= -4)),
            "next2": lambda a, c: y_of(a) == (y_fine(c) >> 1) + side(c),
            "next1": lambda a, c: a == (((c >> 1) + side(c)) & 127),
        }
        for name, hit in hits.items():
            value = 0.5 if name.startswith("lanes") else 1.0
            env.keep_matrix(name, select_matrix(MATRICES[name], hit, value))
        self.env = env
        self.rows4 = select_matrix((16, 32), lambda a, c: (c >> 3) * 4 + ((c & 7) >> 1) == a)
        self.up_rows5 = select_matrix((32, 16), lambda a, c: (a >> 3) * 4 + ((a & 7) >> 1) == c)
        self.up_rows4 = select_matrix((16, 8), lambda a, c: (a >> 1) == c)
        self.up_rows3 = up_rows(16, 16, lambda a: 2 * ix + ((a - 6) >> 1))
        self.up_rows2 = up_rows(24, 16, lambda a: (a >> 1) + 2)
        self.up_rows1 = up_rows(24, 24, lambda a: ((a - 4) >> 1) + 8)

    def kept(self, name):
        return self.env.matrix(name)


def cycle(env):
    m = Math(env)
    iz, ix, iy = env.position
    pick = Selections(ix, iy)
    x_own, b_own = env.load()
    zeros = lambda *s: jnp.zeros(s, jnp.float32)

    mask0 = m.mask(0, 24, 4, 256, 128)
    put0 = lambda v: jnp.concatenate([m.place_rows(v, 4, 24), zeros(24, LANES)], axis=1)
    xc = Field(0, 15, lambda z: put0(x_own[z]))
    bc = Field(0, 15, lambda z: put0(b_own[z]))
    r0 = m.minus_op(bc, xc, mask0, -1, 16)
    u0 = m.correction(r0, mask0, -2, 17)
    p0 = m.minus_op(r0, u0, None, -3, 18)
    coarse = [total([p0(2 * z), p0(2 * z + 1)]) for z in range(-2, 10)]
    coarse = right(coarse, pick.lanes0)
    coarse = left(pick.rows0, coarse)
    mask1c = m.mask(1, 16, 4, 128, 64)
    b1c = field_of(-2, [mask1c(z) * v for z, v in zip(range(-2, 10), coarse)])

    u1 = m.correction(b1c, mask1c, -3, 10)
    p1 = m.minus_op(b1c, u1, None, -4, 11)
    coarse = [total([p1(2 * z), p1(2 * z + 1)]) for z in range(-2, 6)]
    coarse = left(pick.halve_rows, right(coarse, pick.lanes1))
    mask2e = m.mask(2, 8, 2, 128, 32)
    b2c = [mask2e(z) * v for z, v in zip(range(-2, 6), coarse)]

    mask2c = m.mask(2, 16, 4, 128, 32)
    b2p = field_of(-2, [m.place_rows(v, 2, 16) for v in b2c])
    u2 = m.correction(b2p, mask2c, -3, 6)
    p2 = m.minus_op(b2p, u2, None, -4, 7)
    coarse = [total([p2(2 * z), p2(2 * z + 1)]) for z in range(-2, 4)]
    coarse = left(pick.halve_rows, right(coarse, pick.lanes2))
    b3c = total([m.roll(v, 20 * s, 1) for s, v in enumerate(coarse)])

    env.ready()
    env.gather_send("gx3", b3c)
    env.shift_send("fx+", [env.row(x_own, 15)])
    env.shift_send("fx-", [env.row(x_own, 0)])
    env.shift_send("fz+", [x_own[15]])
    env.shift_send("fz-", [x_own[0]])
    lane16 = iota((16, LANES), 1)
    env.shift_send("fy+", m.pack(x_own, 127, 1))
    env.shift_send("fy-", m.pack(x_own, 0, 1))
    packed2 = [total([m.roll(b2c[i], 40 * w + 2, 1) for w, i in enumerate(g)]) for g in GROUPS2]
    for d in (1, -1, 2, -2):
        env.shift_send("x2%+d" % d, packed2)
    env.shift_send("x1+", [m.take_rows(b1c(z), 7, 8) for z in range(-2, 10)])
    env.shift_send("x1-", [m.take_rows(b1c(z), 2, 8) for z in range(-2, 10)])

    row_a, lane_a = iota((16, LANES), 0), iota((16, LANES), 1)
    inside = lambda at: (number(at > 0), number(at < RING - 1))
    (z_lo, z_hi), (x_lo, x_hi), (y_lo, y_hi) = inside(iz), inside(ix), inside(iy)
    row_first, row_last = x_lo * number(row_a == 0), x_hi * number(row_a == 15)
    row_later, row_sooner = number(row_a > 0), number(row_a < 15)
    y_first, y_last = y_lo * number(lane_a == 0), y_hi * number(lane_a == 127)
    y_later, y_sooner = number(lane_a > 0), number(lane_a < 127)
    fx_lo, fx_hi = env.shift_recv("fx+")[0], env.shift_recv("fx-")[0]
    fz_lo, fz_hi = z_lo * env.shift_recv("fz+")[0], z_hi * env.shift_recv("fz-")[0]
    fy_lo, fy_hi = env.shift_recv("fy+")[0], env.shift_recv("fy-")[0]
    r_own = []
    for z in range(16):
        v = x_own[z]
        near = (x_own[z - 1] if z else fz_lo) + (x_own[z + 1] if z < 15 else fz_hi)
        near = near + row_later * m.roll(v, 1, 0) + row_first * fx_lo[z:z + 1]
        near = near + row_sooner * m.roll(v, -1, 0) + row_last * fx_hi[z:z + 1]
        near = near + y_later * m.roll(v, 1, 1) + y_first * m.roll(fy_lo, -z, 1)
        near = near + y_sooner * m.roll(v, -1, 1) + y_last * m.roll(fy_hi, 127 - z, 1)
        r_own.append(b_own[z] - 6.0 * v + near)
    row8 = iota((8, LANES), 0)
    is_low = row8 < 4
    two = lambda a, b: jnp.where(is_low, a, b)
    half = lambda v: m.roll(v, 4, 0)
    env.shift_send("x0+", [two(half(r_own[2 * i][8:]), r_own[2 * i + 1][8:]) for i in range(8)])
    env.shift_send("x0-", [two(r_own[2 * i][:8], half(r_own[2 * i + 1][:8])) for i in range(8)])

    pick.rest(env)

    parts = env.gather_recv("gx3")
    wide = total([m.place_rows(v, 2 * k, 24) for k, v in enumerate(parts)])
    b3x = m.take_rows(wide, 2, 16)

    env.gather_send("gz3", b3x)

    before, after = env.shift_recv("x0+"), env.shift_recv("x0-")
    r0x = []
    for z in range(16):
        low, high = half(r_own[z][:8]), half(r_own[z][8:])
        lo, hi = before[z // 2], after[z // 2]
        if z % 2:
            lo = half(lo)
        else:
            hi = half(hi)
        r0x.append(jnp.concatenate([two(lo, low), two(low, high), two(high, hi)], axis=0))
    env.shift_send("z0+", r0x[12:])
    env.shift_send("z0-", r0x[:4])

    got = {d: env.shift_recv("x2%+d" % d) for d in (1, -1, 2, -2)}
    low, high = number(row8 < 4), number(row8 >= 4)
    b2x = []
    for i in range(3):
        lo = got[1][i] + low * half(got[2][i])
        hi = got[-1][i] + high * half(got[-2][i])
        b2x.append(jnp.concatenate([lo, hi], axis=0) + m.place_rows(packed2[i], 4, 16))
    env.shift_send("z2+1", b2x)
    env.shift_send("z2-1", b2x)
    env.shift_send("z2+2", b2x[2:])
    env.shift_send("z2-2", b2x[:1])

    before, after = env.shift_recv("x1+"), env.shift_recv("x1-")
    b1x = [
        m.place_rows(b1c(i - 2), 4, 24) + m.place_rows(before[i], 3, 24) + m.place_rows(after[i], 14, 24)
        for i in range(12)
    ]
    env.shift_send("z1+", b1x[5:])
    env.shift_send("z1-", b1x[:7])

    r0w = env.shift_recv("z0+") + r0x + env.shift_recv("z0-")
    env.shift_send("y0+", m.pack(r0w, 124, 4))
    env.shift_send("y0-", m.pack(r0w, 0, 4))

    parts = env.gather_recv("gz3")
    lane = iota((16, LANES), 1)
    tiles = []
    for q in range(4):
        tile = None
        for w in range(4):
            z = 4 * q + w
            here = []
            for k in range(RING):
                s = z - 2 * k + 2
                if 0 <= s < 6:
                    here.append(m.roll(parts[k], 32 * w + 6 - 20 * s, 1))
            at = lane - (32 * w + 6)
            part = number((at >= 0) & (at < 20)) * total(here)
            tile = part if tile is None else tile + part
        tiles.append(tile)
    row16, lane512 = iota((16, 512), 0), iota((16, 512), 1)
    slot = lane512 & 31
    y3 = slot - 8 + 16 * iy
    mask3 = number((y3 >= 0) & (y3 < 128))
    not_first, not_last = number(row16 > 0), number(row16 < 15)
    not_bottom, not_top = number(lane512 >= 32), number(lane512 < 480)

    def beside3(v):
        out = not_first * m.roll(v, 1, 0) + not_last * m.roll(v, -1, 0)
        out = out + not_bottom * m.roll(v, 32, 1) + not_top * m.roll(v, -32, 1)
        return out + m.roll(v, 1, 1) + m.roll(v, -1, 1)

    correction3 = lambda r: mask3 * (OWN * r + BETA * beside3(r))
    minus_op3 = lambda b, x: mask3 * (b - 6.0 * x + beside3(x))

    b3s = mask3 * jnp.concatenate(tiles, axis=1)
    p3 = minus_op3(b3s, correction3(b3s))
    b4c = onto(pick.halve_rows, times(p3, pick.kept("lanes3")))

    env.gather_send("gy4", b4c)
    octet = (lane >> 3) & 3
    squeeze = lambda at: total([
        number(octet == q) * m.roll(v, 8 * q - at, 1) for q, v in enumerate(lanes_of(b3s))
    ])
    env.shift_send("y3+", [squeeze(19)])
    env.shift_send("y3-", [squeeze(6)])

    got = {d: env.shift_recv("z2%+d" % d) for d in (1, -1, 2, -2)}
    keep = m.slots(16, 126, 40)

    def plane2(groups, i):
        g = [i in group for group in GROUPS2].index(True)
        return m.roll(groups[g], -(40 * GROUPS2[g].index(i) + 2), 1)

    b2w = []
    for z in range(-5, 9):
        here = []
        if -2 <= z <= 5:
            here.append(plane2(b2x, z + 2))
        if z <= 1:
            here.append(plane2(got[1], z + 6))
        if z >= 2:
            here.append(plane2(got[-1], z - 2))
        if z <= -3:
            here.append(plane2([None, None] + got[2], z + 10))
        if z >= 6:
            here.append(plane2(got[-2], z - 6))
        b2w.append(keep * total(here))
    env.shift_send("y2+", m.pack(b2w, 27))
    env.shift_send("y2-", m.pack(b2w, 126))

    before, after = env.shift_recv("z1+"), env.shift_recv("z1-")
    b1w = []
    for z in range(-5, 13):
        here = []
        if -2 <= z <= 9:
            here.append(b1x[z + 2])
        if z <= 1:
            here.append(before[z + 5])
        if z >= 6:
            here.append(after[z - 6])
        b1w.append(total(here))
    env.shift_send("y1+", m.pack(b1w, 59))
    env.shift_send("y1-", m.pack(b1w, 126))

    mask0 = m.mask(0, 24, 4, 256, 128)
    low = m.unpack(env.shift_recv("y0+"), 24, 124, 4)
    high = m.unpack(env.shift_recv("y0-"), 24, 0, 4)
    r0 = field_of(-4, [
        mask0(i - 4) * jnp.concatenate([v, low[i] + high[i]], axis=1) for i, v in enumerate(r0w)
    ])
    u0 = m.correction(r0, mask0, -3, 18)
    p0 = m.minus_op(r0, u0, None, -2, 17)
    p0 = Field(-2, 17, env.keep("p0", -2, p0))
    near_x = Field(0, 15, lambda z: x_own[z] + m.take_rows(u0(z)[:, :LANES], 4, 16))
    s0 = env.keep("s0", 0, near_x)

    before, after = env.shift_recv("y3+")[0], env.shift_recv("y3-")[0]
    slot16 = lane16 & 31
    low_slot, high_slot = number((slot16 >= 3) & (slot16 < 11)), number((slot16 >= 22) & (slot16 < 30))
    b3w = mask3 * (b3s + jnp.concatenate([
        low_slot * m.roll(before, 3 - 8 * q, 1) + high_slot * m.roll(after, 22 - 8 * q, 1) for q in range(4)
    ], axis=1))
    u3 = correction3(b3w)
    p3 = minus_op3(b3w, u3)
    early_u3, early_p3 = u3, p3
    u3, p3 = env.keep("u3", 0, lambda z: early_u3), env.keep("p3", 0, lambda z: early_p3)

    def window(level, planes, tag, rows, row_off, lo, own_y, at_low, at_high):
        mask = m.mask(level, rows, row_off, LANES, own_y)
        before = m.unpack(env.shift_recv(tag + "+"), len(planes), at_low)
        after = m.unpack(env.shift_recv(tag + "-"), len(planes), at_high)
        return mask, field_of(lo, [
            mask(lo + i) * (v + before[i] + after[i]) for i, v in enumerate(planes)
        ])

    mask2, b2 = window(2, b2w, "y2", 16, 6, -5, 32, 123, 30)
    u2 = m.correction(b2, mask2, -4, 7)
    p2 = m.minus_op(b2, u2, None, -3, 6)
    p2 = Field(-3, 6, env.keep("p2", -3, p2))
    u2 = env.keep("u2", -2, u2)
    mask1, b1 = window(1, b1w, "y1", 24, 8, -5, 64, 123, 62)
    u1 = m.correction(b1, mask1, -4, 11)
    p1 = m.minus_op(b1, u1, None, -3, 10)
    p1 = Field(-3, 10, env.keep("p1", -3, p1))
    u1 = env.keep("u1", -2, u1)
    env.flush()

    parts = env.gather_recv("gy4")
    row, lane = iota((8, LANES), 0), iota((8, LANES), 1)
    keep = []
    for j in range(RING):
        at = lane - (8 * j - 4)
        keep.append(number((at >= 0) & (at < 16) & (lane < 64)))
    b4 = field_of(0, [
        total([keep[j] * m.roll(parts[j], 8 * j - 4 - 16 * z, 1) for j in range(RING)]) for z in range(8)
    ])
    mask4 = number(lane < 64)
    first8, last8 = number(row > 0), number(row < 7)

    def beside4(f, z):
        v = f(z)
        return total([
            f(z - 1), f(z + 1), first8 * m.roll(v, 1, 0), last8 * m.roll(v, -1, 0), m.roll(v, 1, 1), m.roll(v, -1, 1)
        ])

    def correction4(r):
        return Field(0, 7, lambda z: mask4 * (OWN * r(z) + BETA * beside4(r, z)))

    def minus_op4(b, x):
        return Field(0, 7, lambda z: mask4 * (b(z) - 6.0 * x(z) + beside4(x, z)))

    u4 = correction4(b4)
    p4 = minus_op4(b4, u4)
    coarse = jnp.concatenate([p4(2 * z) + p4(2 * z + 1) for z in range(4)], axis=0)
    b5 = onto(pick.rows4, times(coarse, pick.kept("lanes4")))

    row, lane = iota((16, LANES), 0), iota((16, LANES), 1)
    mask5 = number(lane < 32)
    first5, last5 = number((row & 3) > 0), number((row & 3) < 3)
    bottom5, top5 = number(row >= 4), number(row < 12)

    def beside5(v):
        out = first5 * m.roll(v, 1, 0) + last5 * m.roll(v, -1, 0)
        out = out + bottom5 * m.roll(v, 4, 0) + top5 * m.roll(v, -4, 0)
        return out + m.roll(v, 1, 1) + m.roll(v, -1, 1)

    u5 = mask5 * (OWN * b5 + BETA * beside5(b5))
    p5 = mask5 * (b5 - 6.0 * u5 + beside5(u5))
    e5 = u5 + mask5 * (OWN * p5 + BETA * beside5(p5))
    env.coarse_out(e5)

    wide = onto(pick.up_rows5, times(e5, pick.kept("up5")))
    c4 = rows_of(wide, 8)
    c4 = field_of(0, [c4[z // 2] for z in range(8)])
    q4 = minus_op4(p4, c4)
    v4 = correction4(q4)
    e4 = [u4(z) + c4(z) + v4(z) for z in range(8)]

    planes = right(e4, pick.kept("up4"))
    wide = jnp.concatenate([planes[2 * k] + m.roll(planes[2 * k + 1], 64, 1) for k in range(4)], axis=1)
    c3 = mask3 * onto(pick.up_rows4, wide)
    e3 = u3(0) + c3 + correction3(minus_op3(p3(0), c3))

    tiles = lanes_of(onto(pick.up_rows3, e3))
    near = env.window([m.roll(tiles[z // 4], -32 * (z % 4), 1) for z in range(16)])
    inner2, outer2 = widen(*halves(near), pick.kept("up3"), pick.kept("next3"))

    v2 = m.correction(m.minus_op_of_coarse(p2, inner2, outer2, -2, mask2, -3, 6), mask2, -2, 5)
    e2 = [u2(z) + inner2[(z >> 1) + 2] + v2(z) for z in range(-2, 6)]

    inner1, outer1 = widen(*halves(left(pick.up_rows2, e2)), pick.kept("up2"), pick.kept("next2"))
    v1 = m.correction(m.minus_op_of_coarse(p1, inner1, outer1, -2, mask1, -3, 10), mask1, -2, 9)
    e1 = [u1(z) + inner1[(z >> 1) + 2] + v1(z) for z in range(-2, 10)]

    inner0, outer0 = widen(*halves(left(pick.up_rows1, e1)), pick.kept("up1"), pick.kept("next1"))
    q0 = m.minus_op_of_coarse(p0, inner0, outer0, -2, mask0, -2, 17)
    v0 = m.correction(q0, mask0, -1, 16)
    left_over = m.minus_op(q0, v0, None, 0, 15)
    inner = lambda v: m.take_rows(v[:, :LANES], 4, 16)
    for z in range(16):
        env.fine_out(z, s0(z) + inner(inner0[(z >> 1) + 2] + v0(z)), inner(left_over(z)))


class KernelEnv:
    def __init__(self, refs):
        self.refs = refs
        self.position = tuple(lax.axis_index(a) for a in ("gz", "gx", "gy"))
        self.at = dict(zip(("gz", "gx", "gy"), self.position))
        self.started = []
        self.loads = [
            pltpu.make_async_copy(refs["x_in"], refs["previous"], refs["load_sems"].at[0]),
            pltpu.make_async_copy(refs["b_in"], refs["divergence"], refs["load_sems"].at[1]),
        ]
        for load in self.loads:
            load.start()
        self.barrier = pltpu.get_barrier_semaphore()
        for d in (4, 3, 5, 2, 6, 1, 7):
            for axis in ("gx", "gy", "gz"):
                pl.semaphore_signal(
                    self.barrier, inc=1, device_id={axis: self.peer(axis, d)}, device_id_type=pl.DeviceIdType.MESH)

    def peer(self, axis, d):
        return lax.rem(self.at[axis] + (d + RING), RING)

    def roll(self, v, shift, axis):
        return pltpu.roll(v, shift, axis)

    def load(self):
        for load in self.loads:
            load.wait()
        return [[self.refs[n][16 * z:16 * z + 16] for z in range(16)] for n in ("previous", "divergence")]

    def row(self, planes, x):
        return self.refs["previous"][pl.ds(x, 16, stride=16), :]

    def ready(self):
        pl.semaphore_wait(self.barrier, 3 * (RING - 1))

    def copy(self, src, dst, send_sem, recv_sem, axis, d):
        return pltpu.make_async_remote_copy(
            src_ref=src, dst_ref=dst, send_sem=send_sem, recv_sem=recv_sem,
            device_id={axis: self.peer(axis, d)}, device_id_type=pl.DeviceIdType.MESH)

    def shift_copy(self, name):
        axis, d, _, _ = SHIFTS[name]
        i = list(SHIFTS).index(name)
        return self.copy(
            self.refs["out" + name], self.refs["in" + name], self.refs["shift_sems"].at[0, i],
            self.refs["shift_sems"].at[1, i], axis, d)

    def shift_send(self, name, planes):
        ref = self.refs["out" + name]
        for i, v in enumerate(planes):
            ref[i] = v
        copy = self.shift_copy(name)
        copy.start()
        self.started.append(copy)

    def shift_recv(self, name):
        self.shift_copy(name).wait_recv()
        ref = self.refs["in" + name]
        return [ref[i] for i in range(SHIFTS[name][2])]

    def gather_send(self, name, v):
        axis, _ = GATHERS[name]
        i = list(GATHERS).index(name)
        me = self.at[axis]
        buf, src, sems = self.refs["in" + name], self.refs["out" + name], self.refs["gather_sems"]
        src[...] = v
        for d in (4, 3, 5, 2, 6, 1, 7):
            copy = self.copy(src, buf.at[me], sems.at[0, i, d], sems.at[1, i, me], axis, d)
            copy.start()
            self.started.append(copy)
        buf[me] = v

    def gather_recv(self, name):
        axis, _ = GATHERS[name]
        i = list(GATHERS).index(name)
        buf, src, sems = self.refs["in" + name], self.refs["out" + name], self.refs["gather_sems"]
        for d in range(1, RING):
            k = self.peer(axis, d)
            self.copy(src, buf.at[k], sems.at[0, i, d], sems.at[1, i, k], axis, d).wait_recv()
        return [buf[k] for k in range(RING)]

    def window(self, planes):
        ref = self.refs["planes3"]
        zero = jnp.zeros((32, LANES), jnp.float32)
        for z in (0, 1, 18, 19):
            ref[z] = zero
        for z, v in enumerate(planes):
            ref[z + 2] = v
        return [ref[2 * self.position[0] + s] for s in range(6)]

    def keep(self, name, lo, field):
        ref = self.refs["kept_" + name]
        for i in range(KEPT[name][0]):
            ref[i] = field(lo + i)
        return lambda z: ref[z - lo]

    def keep_matrix(self, name, matrix):
        self.refs["matrix_" + name][...] = matrix

    def matrix(self, name):
        return self.refs["matrix_" + name][...]

    def coarse_out(self, v):
        for z in range(4):
            self.refs["coarse"][z] = v[4 * z:4 * z + 4, :32]

    def fine_out(self, z, pressure, residual):
        self.refs["pressure"][z] = pressure
        self.refs["residual"][z] = residual

    def flush(self):
        for copy in self.started:
            copy.wait_send()
        self.started = []


def scratch():
    shapes = {}
    for name, (_, _, count, rows) in SHIFTS.items():
        shapes["out" + name] = pltpu.VMEM((count, rows, LANES), jnp.float32)
        shapes["in" + name] = pltpu.VMEM((count, rows, LANES), jnp.float32)
    for name, (_, rows) in GATHERS.items():
        shapes["out" + name] = pltpu.VMEM((rows, LANES), jnp.float32)
        shapes["in" + name] = pltpu.VMEM((RING, rows, LANES), jnp.float32)
    for name, shape in KEPT.items():
        shapes["kept_" + name] = pltpu.VMEM(shape, jnp.float32)
    for name, shape in MATRICES.items():
        shapes["matrix_" + name] = pltpu.VMEM(shape, jnp.bfloat16)
    shapes["previous"] = pltpu.VMEM((256, LANES), jnp.float32)
    shapes["divergence"] = pltpu.VMEM((256, LANES), jnp.float32)
    shapes["load_sems"] = pltpu.SemaphoreType.DMA((2,))
    shapes["planes3"] = pltpu.VMEM((20, 32, LANES), jnp.float32)
    shapes["shift_sems"] = pltpu.SemaphoreType.DMA((2, len(SHIFTS)))
    shapes["gather_sems"] = pltpu.SemaphoreType.DMA((2, len(GATHERS), RING))
    return shapes


def kernel(names, divergence, previous, pressure, residual, coarse, *buffers):
    refs = dict(zip(names, buffers), x_in=previous, b_in=divergence, pressure=pressure, residual=residual, coarse=coarse)
    env = KernelEnv(refs)
    cycle(env)
    env.flush()


def store_kernel(*refs):
    values, outs, sems = refs[:3], refs[3:6], refs[6]
    copies = [pltpu.make_async_copy(v, o, sems.at[i]) for i, (v, o) in enumerate(zip(values, outs))]
    for copy in copies:
        copy.start()
    for copy in copies:
        copy.wait()


def body(divergence, pressure_prev):
    shapes = scratch()
    block = jax.ShapeDtypeStruct((16, 16, 128), jnp.float32)
    outs = (block, block, jax.ShapeDtypeStruct((4, 4, 32), jnp.float32))
    vmem, hbm = pl.BlockSpec(memory_space=pltpu.VMEM), pl.BlockSpec(memory_space=pltpu.HBM)
    results = pl.pallas_call(
        functools.partial(kernel, tuple(shapes)),
        out_shape=outs,
        in_specs=[hbm, hbm],
        out_specs=(vmem, vmem, vmem),
        scratch_shapes=list(shapes.values()),
        compiler_params=pltpu.CompilerParams(
            collective_id=0, has_side_effects=True, vmem_limit_bytes=48 * 1024 * 1024),
        name="cycle",
    )(*(pltpu.with_memory_space_constraint(v.reshape(256, 128), pltpu.HBM) for v in (divergence, pressure_prev)))
    return pl.pallas_call(
        store_kernel,
        out_shape=outs,
        in_specs=[vmem, vmem, vmem],
        out_specs=(hbm, hbm, hbm),
        scratch_shapes=[pltpu.SemaphoreType.DMA((3,))],
        compiler_params=pltpu.CompilerParams(vmem_limit_bytes=1024 * 1024),
        name="store",
    )(*results)


def solution(mesh):
    in_specs = (P("gz", "gx", "gy"), P("gz", "gx", "gy"))
    out_specs = (P("gz", "gx", "gy"), P("gz", "gx", "gy"), P())
    return jax.shard_map(body, mesh=mesh, in_specs=in_specs, out_specs=out_specs, check_vma=False)
```

```python
import functools

import jax
import jax.numpy as jnp
from jax import lax
from jax.experimental import pallas as pl
from jax.experimental.pallas import tpu as pltpu
from jax.sharding import PartitionSpec as P

FIRST = 1.0 / 7.5
RHO = 1.0 / (2.0 * (5.0 / 3.0) - 0.6)
CARRY = 0.6 * RHO
FRESH = 2.0 * RHO / (0.75 * 6.0)
ALPHA = FIRST * (1.0 + CARRY) + FRESH
BETA = FRESH * FIRST
OWN = ALPHA - 6.0 * BETA

LANES = 128
GROUPS2 = ((0, 1, 2), (3, 4), (5, 6, 7))
RING = 8

SHIFTS = {
    "fx+": ("gx", 1, 1, 16), "fx-": ("gx", -1, 1, 16),
    "fz+": ("gz", 1, 1, 16), "fz-": ("gz", -1, 1, 16),
    "fy+": ("gy", 1, 1, 16), "fy-": ("gy", -1, 1, 16),
    "x0+": ("gx", 1, 8, 8), "x0-": ("gx", -1, 8, 8),
    "x1+": ("gx", 1, 12, 8), "x1-": ("gx", -1, 12, 8),
    "x2+1": ("gx", 1, 3, 8), "x2-1": ("gx", -1, 3, 8),
    "x2+2": ("gx", 2, 3, 8), "x2-2": ("gx", -2, 3, 8),
    "z0+": ("gz", 1, 4, 24), "z0-": ("gz", -1, 4, 24),
    "z1+": ("gz", 1, 7, 24), "z1-": ("gz", -1, 7, 24),
    "z2+1": ("gz", 1, 3, 16), "z2-1": ("gz", -1, 3, 16),
    "z2+2": ("gz", 2, 1, 16), "z2-2": ("gz", -2, 1, 16),
    "y0+": ("gy", 1, 1, 24), "y0-": ("gy", -1, 1, 24),
    "y1+": ("gy", 1, 2, 24), "y1-": ("gy", -1, 2, 24),
    "y2+": ("gy", 1, 1, 16), "y2-": ("gy", -1, 1, 16),
    "y3+": ("gy", 1, 1, 16), "y3-": ("gy", -1, 1, 16),
}
GATHERS = {"gx3": ("gx", 8), "gz3": ("gz", 16), "gy4": ("gy", 8)}


KEPT = {
    "s0": (16, 16, 128), "p0": (20, 24, 256), "u1": (12, 24, 128), "p1": (14, 24, 128),
    "u2": (8, 16, 128), "p2": (10, 16, 128), "u3": (1, 16, 512), "p3": (1, 16, 512),
}
MATRICES = {
    "lanes3": (512, 128), "lanes4": (128, 128), "up5": (128, 128), "up4": (128, 128), "up3": (128, 128),
    "up2": (128, 128), "up1": (128, 256), "next3": (128, 128), "next2": (128, 128), "next1": (128, 256),
    "block4": (128, 128), "block3": (192, 128), "block2": (384, 128), "block1": (576, 384),
}


def iota(shape, dim):
    return lax.broadcasted_iota(jnp.int32, shape, dim)


def number(cond):
    return jnp.where(cond, 1.0, 0.0).astype(jnp.float32)


def parts_of(v):
    high = v.astype(jnp.bfloat16)
    return high, (v - high.astype(jnp.float32)).astype(jnp.bfloat16)


def product(a, b):
    return jnp.dot(a, b, preferred_element_type=jnp.float32)


def times(v, matrix):
    high, low = parts_of(v)
    if v.shape[1] == LANES:
        return product(jnp.concatenate([high, low], axis=1), jnp.concatenate([matrix, matrix], axis=0))
    return product(high, matrix) + product(low, matrix)


def onto(matrix, v):
    high, low = parts_of(v)
    if v.shape[1] == LANES:
        both = product(matrix, jnp.concatenate([high, low], axis=1))
        return both[:, :LANES] + both[:, LANES:]
    return product(matrix, high) + product(matrix, low)


def select_matrix(shape, hit, value=1.0):
    return jnp.where(hit(iota(shape, 0), iota(shape, 1)), value, 0.0).astype(jnp.bfloat16)


def rows_of(stacked, rows):
    return [stacked[i * rows:(i + 1) * rows] for i in range(stacked.shape[0] // rows)]


def lanes_of(stacked):
    return [stacked[:, i * LANES:(i + 1) * LANES] for i in range(stacked.shape[1] // LANES)]


def right(planes, matrix):
    return rows_of(times(jnp.concatenate(planes, axis=0), matrix), planes[0].shape[0])


def left(matrix, planes):
    return lanes_of(onto(matrix, jnp.concatenate(planes, axis=1)))


def twice(matrix):
    return jnp.concatenate([matrix, matrix], axis=0)


def spread_rows(planes, block):
    stacked = jnp.concatenate(planes, axis=0)
    missing = block.shape[1] - stacked.shape[0]
    if missing:
        stacked = jnp.concatenate([stacked, jnp.zeros((missing, LANES), jnp.float32)], axis=0)
    return product(block, jnp.concatenate(parts_of(stacked), axis=1)).astype(jnp.bfloat16)


def widen(planes, rows, block, up, following):
    both = spread_rows(planes, block)
    half = both.shape[0] // 2
    own, beside = both[:half], both[half:]
    outer = product(beside, twice(up)) + product(own, twice(following))
    return rows_of(product(own, twice(up)), rows), rows_of(outer, rows)


def total(terms):
    terms = [t for t in terms if t is not None]
    out = terms[0]
    for t in terms[1:]:
        out = out + t
    return out


class Field:
    def __init__(self, lo, hi, make):
        self.lo, self.hi, self.make, self.have = lo, hi, make, {}

    def __call__(self, z):
        if z < self.lo or z > self.hi:
            return None
        if z not in self.have:
            self.have[z] = self.make(z)
        return self.have[z]


def field_of(lo, planes):
    return Field(lo, lo + len(planes) - 1, lambda z: planes[z - lo])


class Math:
    def __init__(self, env):
        self.env = env
        self.iz, self.ix, self.iy = env.position

    def roll(self, v, shift, axis):
        shift = shift % v.shape[axis]
        return v if shift == 0 else self.env.roll(v, shift, axis)

    def place_rows(self, v, at, rows):
        pad = jnp.zeros((rows - v.shape[0],) + v.shape[1:], v.dtype)
        return self.roll(jnp.concatenate([v, pad], axis=0), at, 0)

    def take_rows(self, v, at, rows):
        return self.roll(v, -at, 0)[:rows]

    def mask(self, level, rows, row_off, lanes, own_y):
        nz, nx, ny = 16 >> level, 16 >> level, 128 >> level
        x = iota((rows, lanes), 0) - row_off + self.ix * nx
        lane = iota((rows, lanes), 1)
        y = jnp.where(lane < (own_y + lanes) // 2, lane, lane - lanes) + self.iy * ny
        flat = number((x >= 0) & (x < 128 >> level) & (y >= 0) & (y < 1024 >> level))

        def make(z):
            if 0 <= z < nz:
                return flat
            at = self.iz * nz + z
            return flat * number((at >= 0) & (at < 128 >> level))

        return Field(-16, 32, make)

    def beside(self, f, z):
        v = f(z)
        terms = [f(z - 1), f(z + 1)]
        if v is not None:
            terms += [self.roll(v, 1, 0), self.roll(v, -1, 0), self.roll(v, 1, 1), self.roll(v, -1, 1)]
        return total(terms)

    def correction(self, r, mask, lo, hi):
        def make(z):
            v = r(z)
            near = BETA * self.beside(r, z)
            return mask(z) * (near if v is None else OWN * v + near)
        return Field(lo, hi, make)

    def minus_op(self, b, x, mask, lo, hi):
        def make(z):
            out = self.beside(x, z)
            if x(z) is not None:
                out = out - 6.0 * x(z)
            if b(z) is not None:
                out = out + b(z)
            return out if mask is None else mask(z) * out
        return Field(lo, hi, make)

    def minus_op_of_coarse(self, b, inner, outer, lo_coarse, mask, lo, hi):
        def make(z):
            at = (z >> 1) - lo_coarse
            return mask(z) * (b(z) + outer[at] + inner[at + 2 * (z & 1) - 1] - 3.0 * inner[at])
        return Field(lo, hi, make)

    def slots(self, rows, start, width):
        lane = (iota((rows, LANES), 1) - start) & (LANES - 1)
        return number(lane < width)

    def pack(self, planes, start, width=8):
        rows, per = planes[0].shape[0], LANES // width
        tiles = []
        for g in range(0, len(planes), per):
            tiles.append(total([
                self.slots(rows, width * w, width) * self.roll(plane, width * w - start, 1)
                for w, plane in enumerate(planes[g:g + per])
            ]))
        return tiles

    def unpack(self, tiles, count, start, width=8):
        keep, per = self.slots(tiles[0].shape[0], start, width), LANES // width
        return [keep * self.roll(tiles[i // per], start - width * (i % per), 1) for i in range(count)]


class Selections:
    def __init__(self, ix, iy):
        self.lanes0 = select_matrix((256, 128), lambda a, c: (a >> 1) == c, 0.5)
        self.rows0 = select_matrix((16, 24), lambda a, c: (c >> 1) + 2 == a)
        self.lanes1 = select_matrix((128, 128), lambda a, c: (a >> 1) + jnp.where(a >= 96, 64, 0) == c, 0.5)
        self.halve_rows = select_matrix((8, 16), lambda a, c: (c >> 1) == a)
        self.lanes2 = select_matrix((128, 128), lambda a, c: (jnp.where(a < 80, a, a - 128) >> 1) + 2 == c, 0.5)
        self.ix, self.iy = ix, iy

    def rest(self, env):
        ix, iy = self.ix, self.iy
        y_of = lambda c: jnp.where(c < 80, c, c - 128)
        y_fine = lambda c: jnp.where(c < 96, c, c - 128)
        side = lambda c: 2 * (c & 1) - 1

        def blocks(rows, depth, count, coarse, kinds=2):
            shape = (rows, -(-count * depth // LANES) * LANES)
            fine, column = iota(shape, 0), iota(shape, 1)
            out = []
            for kind in range(kinds):
                want = coarse(fine) + kind * side(fine)
                gap = column - jnp.where((want >= 0) & (want < depth), want, 4096)
                out += [number(gap == depth * k) for k in range(count)]
            return jnp.concatenate(out, axis=0).astype(jnp.bfloat16)

        env.keep_matrix("block4", blocks(16, 8, 8, lambda a: a >> 1, 1))
        env.keep_matrix("block3", blocks(16, 16, 6, lambda a: 2 * ix + ((a - 6) >> 1)))
        env.keep_matrix("block2", blocks(24, 16, 8, lambda a: (a >> 1) + 2))
        env.keep_matrix("block1", blocks(24, 24, 12, lambda a: ((a - 4) >> 1) + 8))
        hits = {
            "lanes3": lambda a, c: 16 * (a >> 6) + ((a & 31) >> 1) == c,
            "lanes4": lambda a, c: ((a >> 1) == c) & (a < 64),
            "up5": lambda a, c: (a == (c >> 1)) & (c < 64),
            "up4": lambda a, c: (a == 8 * iy + (((c & 31) - 8) >> 1)) & (c < 64),
            "up3": lambda a, c: (a - 8 == (y_of(c) >> 1)) & (a < 32) & (y_of(c) < 36) & (y_of(c) >= -4),
            "up2": lambda a, c: y_of(a) == (y_fine(c) >> 1),
            "up1": lambda a, c: a == (c >> 1),
            "next3": lambda a, c: (
                (a - 8 == (y_of(c) >> 1) + side(c)) & (a < 32) & (y_of(c) < 36) & (y_of(c) >= -4)),
            "next2": lambda a, c: y_of(a) == (y_fine(c) >> 1) + side(c),
            "next1": lambda a, c: a == (((c >> 1) + side(c)) & 127),
        }
        for name, hit in hits.items():
            value = 0.5 if name.startswith("lanes") else 1.0
            env.keep_matrix(name, select_matrix(MATRICES[name], hit, value))
        self.env = env
        self.rows4 = select_matrix((16, 32), lambda a, c: (c >> 3) * 4 + ((c & 7) >> 1) == a)
        self.up_rows5 = select_matrix((32, 16), lambda a, c: (a >> 3) * 4 + ((a & 7) >> 1) == c)

    def kept(self, name):
        return self.env.matrix(name)


def cycle(env):
    m = Math(env)
    iz, ix, iy = env.position
    pick = Selections(ix, iy)
    x_own, b_own = env.load()
    zeros = lambda *s: jnp.zeros(s, jnp.float32)

    mask0 = m.mask(0, 24, 4, 256, 128)
    put0 = lambda v: jnp.concatenate([m.place_rows(v, 4, 24), zeros(24, LANES)], axis=1)
    xc = Field(0, 15, lambda z: put0(x_own[z]))
    bc = Field(0, 15, lambda z: put0(b_own[z]))
    r0 = m.minus_op(bc, xc, mask0, -1, 16)
    u0 = m.correction(r0, mask0, -2, 17)
    p0 = m.minus_op(r0, u0, None, -3, 18)
    coarse = [total([p0(2 * z), p0(2 * z + 1)]) for z in range(-2, 10)]
    coarse = right(coarse, pick.lanes0)
    coarse = left(pick.rows0, coarse)
    mask1c = m.mask(1, 16, 4, 128, 64)
    b1c = field_of(-2, [mask1c(z) * v for z, v in zip(range(-2, 10), coarse)])

    u1 = m.correction(b1c, mask1c, -3, 10)
    p1 = m.minus_op(b1c, u1, None, -4, 11)
    coarse = [total([p1(2 * z), p1(2 * z + 1)]) for z in range(-2, 6)]
    coarse = left(pick.halve_rows, right(coarse, pick.lanes1))
    mask2e = m.mask(2, 8, 2, 128, 32)
    b2c = [mask2e(z) * v for z, v in zip(range(-2, 6), coarse)]

    mask2c = m.mask(2, 16, 4, 128, 32)
    b2p = field_of(-2, [m.place_rows(v, 2, 16) for v in b2c])
    u2 = m.correction(b2p, mask2c, -3, 6)
    p2 = m.minus_op(b2p, u2, None, -4, 7)
    coarse = [total([p2(2 * z), p2(2 * z + 1)]) for z in range(-2, 4)]
    coarse = left(pick.halve_rows, right(coarse, pick.lanes2))
    b3c = total([m.roll(v, 20 * s, 1) for s, v in enumerate(coarse)])

    env.ready()
    env.gather_send("gx3", b3c)
    env.shift_send("fx+", [env.row(x_own, 15)])
    env.shift_send("fx-", [env.row(x_own, 0)])
    env.shift_send("fz+", [x_own[15]])
    env.shift_send("fz-", [x_own[0]])
    lane16 = iota((16, LANES), 1)
    env.shift_send("fy+", m.pack(x_own, 127, 1))
    env.shift_send("fy-", m.pack(x_own, 0, 1))
    packed2 = [total([m.roll(b2c[i], 40 * w + 2, 1) for w, i in enumerate(g)]) for g in GROUPS2]
    for d in (1, -1, 2, -2):
        env.shift_send("x2%+d" % d, packed2)
    env.shift_send("x1+", [m.take_rows(b1c(z), 7, 8) for z in range(-2, 10)])
    env.shift_send("x1-", [m.take_rows(b1c(z), 2, 8) for z in range(-2, 10)])

    row_a, lane_a = iota((16, LANES), 0), iota((16, LANES), 1)
    inside = lambda at: (number(at > 0), number(at < RING - 1))
    (z_lo, z_hi), (x_lo, x_hi), (y_lo, y_hi) = inside(iz), inside(ix), inside(iy)
    row_first, row_last = x_lo * number(row_a == 0), x_hi * number(row_a == 15)
    row_later, row_sooner = number(row_a > 0), number(row_a < 15)
    y_first, y_last = y_lo * number(lane_a == 0), y_hi * number(lane_a == 127)
    y_later, y_sooner = number(lane_a > 0), number(lane_a < 127)
    fx_lo, fx_hi = env.shift_recv("fx+")[0], env.shift_recv("fx-")[0]
    fz_lo, fz_hi = z_lo * env.shift_recv("fz+")[0], z_hi * env.shift_recv("fz-")[0]
    fy_lo, fy_hi = env.shift_recv("fy+")[0], env.shift_recv("fy-")[0]
    r_own = []
    for z in range(16):
        v = x_own[z]
        near = (x_own[z - 1] if z else fz_lo) + (x_own[z + 1] if z < 15 else fz_hi)
        near = near + row_later * m.roll(v, 1, 0) + row_first * fx_lo[z:z + 1]
        near = near + row_sooner * m.roll(v, -1, 0) + row_last * fx_hi[z:z + 1]
        near = near + y_later * m.roll(v, 1, 1) + y_first * m.roll(fy_lo, -z, 1)
        near = near + y_sooner * m.roll(v, -1, 1) + y_last * m.roll(fy_hi, 127 - z, 1)
        r_own.append(b_own[z] - 6.0 * v + near)
    row8 = iota((8, LANES), 0)
    is_low = row8 < 4
    two = lambda a, b: jnp.where(is_low, a, b)
    half = lambda v: m.roll(v, 4, 0)
    env.shift_send("x0+", [two(half(r_own[2 * i][8:]), r_own[2 * i + 1][8:]) for i in range(8)])
    env.shift_send("x0-", [two(r_own[2 * i][:8], half(r_own[2 * i + 1][:8])) for i in range(8)])

    pick.rest(env)

    parts = env.gather_recv("gx3")
    wide = total([m.place_rows(v, 2 * k, 24) for k, v in enumerate(parts)])
    b3x = m.take_rows(wide, 2, 16)

    env.gather_send("gz3", b3x)

    before, after = env.shift_recv("x0+"), env.shift_recv("x0-")
    r0x = []
    for z in range(16):
        low, high = half(r_own[z][:8]), half(r_own[z][8:])
        lo, hi = before[z // 2], after[z // 2]
        if z % 2:
            lo = half(lo)
        else:
            hi = half(hi)
        r0x.append(jnp.concatenate([two(lo, low), two(low, high), two(high, hi)], axis=0))
    env.shift_send("z0+", r0x[12:])
    env.shift_send("z0-", r0x[:4])

    got = {d: env.shift_recv("x2%+d" % d) for d in (1, -1, 2, -2)}
    low, high = number(row8 < 4), number(row8 >= 4)
    b2x = []
    for i in range(3):
        lo = got[1][i] + low * half(got[2][i])
        hi = got[-1][i] + high * half(got[-2][i])
        b2x.append(jnp.concatenate([lo, hi], axis=0) + m.place_rows(packed2[i], 4, 16))
    env.shift_send("z2+1", b2x)
    env.shift_send("z2-1", b2x)
    env.shift_send("z2+2", b2x[2:])
    env.shift_send("z2-2", b2x[:1])

    before, after = env.shift_recv("x1+"), env.shift_recv("x1-")
    b1x = [
        m.place_rows(b1c(i - 2), 4, 24) + m.place_rows(before[i], 3, 24) + m.place_rows(after[i], 14, 24)
        for i in range(12)
    ]
    env.shift_send("z1+", b1x[5:])
    env.shift_send("z1-", b1x[:7])

    parts = env.gather_recv("gz3")
    lane = iota((16, LANES), 1)
    tiles = []
    for q in range(4):
        tile = None
        for w in range(4):
            z = 4 * q + w
            here = []
            for k in range(RING):
                s = z - 2 * k + 2
                if 0 <= s < 6:
                    here.append(m.roll(parts[k], 32 * w + 6 - 20 * s, 1))
            at = lane - (32 * w + 6)
            part = number((at >= 0) & (at < 20)) * total(here)
            tile = part if tile is None else tile + part
        tiles.append(tile)
    row16, lane512 = iota((16, 512), 0), iota((16, 512), 1)
    slot = lane512 & 31
    y3 = slot - 8 + 16 * iy
    mask3 = number((y3 >= 0) & (y3 < 128))
    not_first, not_last = number(row16 > 0), number(row16 < 15)
    not_bottom, not_top = number(lane512 >= 32), number(lane512 < 480)

    def beside3(v):
        out = not_first * m.roll(v, 1, 0) + not_last * m.roll(v, -1, 0)
        out = out + not_bottom * m.roll(v, 32, 1) + not_top * m.roll(v, -32, 1)
        return out + m.roll(v, 1, 1) + m.roll(v, -1, 1)

    correction3 = lambda r: mask3 * (OWN * r + BETA * beside3(r))
    minus_op3 = lambda b, x: mask3 * (b - 6.0 * x + beside3(x))

    b3s = mask3 * jnp.concatenate(tiles, axis=1)
    p3 = minus_op3(b3s, correction3(b3s))
    b4c = onto(pick.halve_rows, times(p3, pick.kept("lanes3")))

    env.gather_send("gy4", b4c)
    octet = (lane >> 3) & 3
    squeeze = lambda at: total([
        number(octet == q) * m.roll(v, 8 * q - at, 1) for q, v in enumerate(lanes_of(b3s))
    ])
    env.shift_send("y3+", [squeeze(19)])
    env.shift_send("y3-", [squeeze(6)])

    r0w = env.shift_recv("z0+") + r0x + env.shift_recv("z0-")
    env.shift_send("y0+", m.pack(r0w, 124, 4))
    env.shift_send("y0-", m.pack(r0w, 0, 4))

    got = {d: env.shift_recv("z2%+d" % d) for d in (1, -1, 2, -2)}
    keep = m.slots(16, 126, 40)

    def plane2(groups, i):
        g = [i in group for group in GROUPS2].index(True)
        return m.roll(groups[g], -(40 * GROUPS2[g].index(i) + 2), 1)

    b2w = []
    for z in range(-5, 9):
        here = []
        if -2 <= z <= 5:
            here.append(plane2(b2x, z + 2))
        if z <= 1:
            here.append(plane2(got[1], z + 6))
        if z >= 2:
            here.append(plane2(got[-1], z - 2))
        if z <= -3:
            here.append(plane2([None, None] + got[2], z + 10))
        if z >= 6:
            here.append(plane2(got[-2], z - 6))
        b2w.append(keep * total(here))
    env.shift_send("y2+", m.pack(b2w, 27))
    env.shift_send("y2-", m.pack(b2w, 126))

    before, after = env.shift_recv("z1+"), env.shift_recv("z1-")
    b1w = []
    for z in range(-5, 13):
        here = []
        if -2 <= z <= 9:
            here.append(b1x[z + 2])
        if z <= 1:
            here.append(before[z + 5])
        if z >= 6:
            here.append(after[z - 6])
        b1w.append(total(here))
    env.shift_send("y1+", m.pack(b1w, 59))
    env.shift_send("y1-", m.pack(b1w, 126))

    kept = {}
    before0, after0 = env.shift_recv("y0+"), env.shift_recv("y0-")

    def finest():
        mask = m.mask(0, 24, 4, 256, 128)
        low, high = m.unpack(before0, 24, 124, 4), m.unpack(after0, 24, 0, 4)
        r = field_of(-4, [
            mask(i - 4) * jnp.concatenate([v, low[i] + high[i]], axis=1) for i, v in enumerate(r0w)
        ])
        u = m.correction(r, mask, -3, 18)
        kept["p0"] = env.keep("p0", -2, m.minus_op(r, u, None, -2, 17))
        near_x = Field(0, 15, lambda z: x_own[z] + m.take_rows(u(z)[:, :LANES], 4, 16))
        kept["s0"] = env.keep("s0", 0, near_x)

    env.region(finest)

    mask0 = m.mask(0, 24, 4, 256, 128)
    mask1 = m.mask(1, 24, 8, LANES, 64)
    mask2 = m.mask(2, 16, 6, LANES, 32)
    env.flush()

    parts = env.gather_recv("gy4")
    row, lane = iota((8, LANES), 0), iota((8, LANES), 1)
    keep = []
    for j in range(RING):
        at = lane - (8 * j - 4)
        keep.append(number((at >= 0) & (at < 16) & (lane < 64)))
    b4 = field_of(0, [
        total([keep[j] * m.roll(parts[j], 8 * j - 4 - 16 * z, 1) for j in range(RING)]) for z in range(8)
    ])
    mask4 = number(lane < 64)
    first8, last8 = number(row > 0), number(row < 7)

    def beside4(f, z):
        v = f(z)
        return total([
            f(z - 1), f(z + 1), first8 * m.roll(v, 1, 0), last8 * m.roll(v, -1, 0), m.roll(v, 1, 1), m.roll(v, -1, 1)
        ])

    def correction4(r):
        return Field(0, 7, lambda z: mask4 * (OWN * r(z) + BETA * beside4(r, z)))

    def minus_op4(b, x):
        return Field(0, 7, lambda z: mask4 * (b(z) - 6.0 * x(z) + beside4(x, z)))

    u4 = correction4(b4)
    p4 = minus_op4(b4, u4)
    coarse = jnp.concatenate([p4(2 * z) + p4(2 * z + 1) for z in range(4)], axis=0)
    b5 = onto(pick.rows4, times(coarse, pick.kept("lanes4")))

    row, lane = iota((16, LANES), 0), iota((16, LANES), 1)
    mask5 = number(lane < 32)
    first5, last5 = number((row & 3) > 0), number((row & 3) < 3)
    bottom5, top5 = number(row >= 4), number(row < 12)

    def beside5(v):
        out = first5 * m.roll(v, 1, 0) + last5 * m.roll(v, -1, 0)
        out = out + bottom5 * m.roll(v, 4, 0) + top5 * m.roll(v, -4, 0)
        return out + m.roll(v, 1, 1) + m.roll(v, -1, 1)

    u5 = mask5 * (OWN * b5 + BETA * beside5(b5))
    p5 = mask5 * (b5 - 6.0 * u5 + beside5(u5))
    e5 = u5 + mask5 * (OWN * p5 + BETA * beside5(p5))
    env.coarse_out(e5)

    sides = {tag: (env.shift_recv(tag + "+"), env.shift_recv(tag + "-")) for tag in ("y3", "y2", "y1")}

    def window(level, planes, tag, rows, row_off, lo, own_y, at_low, at_high):
        mask = m.mask(level, rows, row_off, LANES, own_y)
        before = m.unpack(sides[tag][0], len(planes), at_low)
        after = m.unpack(sides[tag][1], len(planes), at_high)
        return mask, field_of(lo, [
            mask(lo + i) * (v + before[i] + after[i]) for i, v in enumerate(planes)
        ])

    def coarser():
        before, after = sides["y3"][0][0], sides["y3"][1][0]
        slot16 = lane16 & 31
        low_slot, high_slot = number((slot16 >= 3) & (slot16 < 11)), number((slot16 >= 22) & (slot16 < 30))
        b = mask3 * (b3s + jnp.concatenate([
            low_slot * m.roll(before, 3 - 8 * q, 1) + high_slot * m.roll(after, 22 - 8 * q, 1) for q in range(4)
        ], axis=1))
        u = correction3(b)
        kept["u3"], kept["p3"] = env.keep("u3", 0, lambda z: u), env.keep("p3", 0, lambda z: minus_op3(b, u))
        mask, b2 = window(2, b2w, "y2", 16, 6, -5, 32, 123, 30)
        u2 = m.correction(b2, mask, -4, 7)
        kept["p2"] = env.keep("p2", -3, m.minus_op(b2, u2, None, -3, 6))
        kept["u2"] = env.keep("u2", -2, u2)
        mask, b1 = window(1, b1w, "y1", 24, 8, -5, 64, 123, 62)
        u1 = m.correction(b1, mask, -4, 11)
        kept["p1"] = env.keep("p1", -3, m.minus_op(b1, u1, None, -3, 10))
        kept["u1"] = env.keep("u1", -2, u1)

    coarser()
    s0, u1, u2, u3, p3 = (kept[name] for name in ("s0", "u1", "u2", "u3", "p3"))
    p0, p1, p2 = Field(-2, 17, kept["p0"]), Field(-3, 10, kept["p1"]), Field(-3, 6, kept["p2"])

    wide = product(spread_rows([e5], pick.up_rows5), twice(pick.kept("up5")))
    c4 = rows_of(wide, 8)
    c4 = field_of(0, [c4[z // 2] for z in range(8)])
    q4 = minus_op4(p4, c4)
    v4 = correction4(q4)
    e4 = [u4(z) + c4(z) + v4(z) for z in range(8)]

    planes = rows_of(product(spread_rows(e4, pick.kept("block4")), twice(pick.kept("up4"))), 16)
    c3 = mask3 * jnp.concatenate([planes[2 * k] + m.roll(planes[2 * k + 1], 64, 1) for k in range(4)], axis=1)
    e3 = u3(0) + c3 + correction3(minus_op3(p3(0), c3))

    tiles = lanes_of(e3)
    near = env.window([m.roll(tiles[z // 4], -32 * (z % 4), 1) for z in range(16)])
    inner2, outer2 = widen(near, 16, pick.kept("block3"), pick.kept("up3"), pick.kept("next3"))

    v2 = m.correction(m.minus_op_of_coarse(p2, inner2, outer2, -2, mask2, -3, 6), mask2, -2, 5)
    e2 = [u2(z) + inner2[(z >> 1) + 2] + v2(z) for z in range(-2, 6)]

    inner1, outer1 = widen(e2, 24, pick.kept("block2"), pick.kept("up2"), pick.kept("next2"))
    v1 = m.correction(m.minus_op_of_coarse(p1, inner1, outer1, -2, mask1, -3, 10), mask1, -2, 9)
    e1 = [u1(z) + inner1[(z >> 1) + 2] + v1(z) for z in range(-2, 10)]

    inner0, outer0 = widen(e1, 24, pick.kept("block1"), pick.kept("up1"), pick.kept("next1"))
    q0 = m.minus_op_of_coarse(p0, inner0, outer0, -2, mask0, -2, 17)
    v0 = m.correction(q0, mask0, -1, 16)
    left_over = m.minus_op(q0, v0, None, 0, 15)
    inner = lambda v: m.take_rows(v[:, :LANES], 4, 16)
    for z in range(16):
        env.fine_out(z, s0(z) + inner(inner0[(z >> 1) + 2] + v0(z)), inner(left_over(z)))


class KernelEnv:
    def __init__(self, refs):
        self.refs = refs
        self.position = tuple(lax.axis_index(a) for a in ("gz", "gx", "gy"))
        self.at = dict(zip(("gz", "gx", "gy"), self.position))
        self.started = []
        self.loads = [
            pltpu.make_async_copy(refs["x_in"], refs["previous"], refs["load_sems"].at[0]),
            pltpu.make_async_copy(refs["b_in"], refs["divergence"], refs["load_sems"].at[1]),
        ]
        for load in self.loads:
            load.start()
        self.barrier = pltpu.get_barrier_semaphore()
        for d in (4, 3, 5, 2, 6, 1, 7):
            for axis in ("gx", "gy", "gz"):
                pl.semaphore_signal(
                    self.barrier, inc=1, device_id={axis: self.peer(axis, d)}, device_id_type=pl.DeviceIdType.MESH)

    def peer(self, axis, d):
        return lax.rem(self.at[axis] + (d + RING), RING)

    def roll(self, v, shift, axis):
        return pltpu.roll(v, shift, axis)

    def load(self):
        for load in self.loads:
            load.wait()
        return [[self.refs[n][16 * z:16 * z + 16] for z in range(16)] for n in ("previous", "divergence")]

    def row(self, planes, x):
        return self.refs["previous"][pl.ds(x, 16, stride=16), :]

    def ready(self):
        pl.semaphore_wait(self.barrier, 3 * (RING - 1))

    def copy(self, src, dst, send_sem, recv_sem, axis, d):
        return pltpu.make_async_remote_copy(
            src_ref=src, dst_ref=dst, send_sem=send_sem, recv_sem=recv_sem,
            device_id={axis: self.peer(axis, d)}, device_id_type=pl.DeviceIdType.MESH)

    def shift_copy(self, name):
        axis, d, _, _ = SHIFTS[name]
        i = list(SHIFTS).index(name)
        return self.copy(
            self.refs["out" + name], self.refs["in" + name], self.refs["shift_sems"].at[0, i],
            self.refs["shift_sems"].at[1, i], axis, d)

    def shift_send(self, name, planes):
        ref = self.refs["out" + name]
        for i, v in enumerate(planes):
            ref[i] = v
        copy = self.shift_copy(name)
        copy.start()
        self.started.append(copy)

    def shift_recv(self, name):
        self.shift_copy(name).wait_recv()
        ref = self.refs["in" + name]
        return [ref[i] for i in range(SHIFTS[name][2])]

    def gather_send(self, name, v):
        axis, _ = GATHERS[name]
        i = list(GATHERS).index(name)
        me = self.at[axis]
        buf, src, sems = self.refs["in" + name], self.refs["out" + name], self.refs["gather_sems"]
        src[...] = v
        for d in (4, 3, 5, 2, 6, 1, 7):
            copy = self.copy(src, buf.at[me], sems.at[0, i, d], sems.at[1, i, me], axis, d)
            copy.start()
            self.started.append(copy)
        buf[me] = v

    def gather_recv(self, name):
        axis, _ = GATHERS[name]
        i = list(GATHERS).index(name)
        buf, src, sems = self.refs["in" + name], self.refs["out" + name], self.refs["gather_sems"]
        for d in range(1, RING):
            k = self.peer(axis, d)
            self.copy(src, buf.at[k], sems.at[0, i, d], sems.at[1, i, k], axis, d).wait_recv()
        return [buf[k] for k in range(RING)]

    def window(self, planes):
        ref = self.refs["planes3"]
        zero = jnp.zeros((16, LANES), jnp.float32)
        for z in (0, 1, 18, 19):
            ref[z] = zero
        for z, v in enumerate(planes):
            ref[z + 2] = v
        return [ref[2 * self.position[0] + s] for s in range(6)]

    def region(self, work):
        pl.when(self.position[0] < RING)(work)

    def keep(self, name, lo, field):
        ref = self.refs["kept_" + name]
        for i in range(KEPT[name][0]):
            ref[i] = field(lo + i)
        return lambda z: ref[z - lo]

    def keep_matrix(self, name, matrix):
        self.refs["matrix_" + name][...] = matrix

    def matrix(self, name):
        return self.refs["matrix_" + name][...]

    def coarse_out(self, v):
        for z in range(4):
            self.refs["coarse"][z] = v[4 * z:4 * z + 4, :32]

    def fine_out(self, z, pressure, residual):
        self.refs["pressure"][z] = pressure
        self.refs["residual"][z] = residual

    def flush(self):
        for copy in self.started:
            copy.wait_send()
        self.started = []


def scratch():
    shapes = {}
    for name, (_, _, count, rows) in SHIFTS.items():
        shapes["out" + name] = pltpu.VMEM((count, rows, LANES), jnp.float32)
        shapes["in" + name] = pltpu.VMEM((count, rows, LANES), jnp.float32)
    for name, (_, rows) in GATHERS.items():
        shapes["out" + name] = pltpu.VMEM((rows, LANES), jnp.float32)
        shapes["in" + name] = pltpu.VMEM((RING, rows, LANES), jnp.float32)
    for name, shape in KEPT.items():
        shapes["kept_" + name] = pltpu.VMEM(shape, jnp.float32)
    for name, shape in MATRICES.items():
        shapes["matrix_" + name] = pltpu.VMEM(shape, jnp.bfloat16)
    shapes["previous"] = pltpu.VMEM((256, LANES), jnp.float32)
    shapes["divergence"] = pltpu.VMEM((256, LANES), jnp.float32)
    shapes["load_sems"] = pltpu.SemaphoreType.DMA((2,))
    shapes["planes3"] = pltpu.VMEM((20, 16, LANES), jnp.float32)
    shapes["shift_sems"] = pltpu.SemaphoreType.DMA((2, len(SHIFTS)))
    shapes["gather_sems"] = pltpu.SemaphoreType.DMA((2, len(GATHERS), RING))
    return shapes


def kernel(names, divergence, previous, pressure, residual, coarse, *buffers):
    refs = dict(zip(names, buffers), x_in=previous, b_in=divergence, pressure=pressure, residual=residual, coarse=coarse)
    env = KernelEnv(refs)
    cycle(env)
    env.flush()


def store_kernel(*refs):
    values, outs, sems = refs[:3], refs[3:6], refs[6]
    copies = [pltpu.make_async_copy(v, o, sems.at[i]) for i, (v, o) in enumerate(zip(values, outs))]
    for copy in copies:
        copy.start()
    for copy in copies:
        copy.wait()


def body(divergence, pressure_prev):
    shapes = scratch()
    block = jax.ShapeDtypeStruct((16, 16, 128), jnp.float32)
    outs = (block, block, jax.ShapeDtypeStruct((4, 4, 32), jnp.float32))
    vmem, hbm = pl.BlockSpec(memory_space=pltpu.VMEM), pl.BlockSpec(memory_space=pltpu.HBM)
    results = pl.pallas_call(
        functools.partial(kernel, tuple(shapes)),
        out_shape=outs,
        in_specs=[hbm, hbm],
        out_specs=(vmem, vmem, vmem),
        scratch_shapes=list(shapes.values()),
        compiler_params=pltpu.CompilerParams(
            collective_id=0, has_side_effects=True, vmem_limit_bytes=48 * 1024 * 1024),
        name="cycle",
    )(*(pltpu.with_memory_space_constraint(v.reshape(256, 128), pltpu.HBM) for v in (divergence, pressure_prev)))
    return pl.pallas_call(
        store_kernel,
        out_shape=outs,
        in_specs=[vmem, vmem, vmem],
        out_specs=(hbm, hbm, hbm),
        scratch_shapes=[pltpu.SemaphoreType.DMA((3,))],
        compiler_params=pltpu.CompilerParams(vmem_limit_bytes=1024 * 1024),
        name="store",
    )(*results)


def solution(mesh):
    in_specs = (P("gz", "gx", "gy"), P("gz", "gx", "gy"))
    out_specs = (P("gz", "gx", "gy"), P("gz", "gx", "gy"), P())
    return jax.shard_map(body, mesh=mesh, in_specs=in_specs, out_specs=out_specs, check_vma=False)
```

```python
import functools

import jax
import jax.numpy as jnp
from jax import lax
from jax.experimental import pallas as pl
from jax.experimental.pallas import tpu as pltpu
from jax.sharding import PartitionSpec as P

FIRST = 1.0 / 7.5
RHO = 1.0 / (2.0 * (5.0 / 3.0) - 0.6)
CARRY = 0.6 * RHO
FRESH = 2.0 * RHO / (0.75 * 6.0)
ALPHA = FIRST * (1.0 + CARRY) + FRESH
BETA = FRESH * FIRST
OWN = ALPHA - 6.0 * BETA

LANES = 128
GROUPS2 = ((0, 1, 2), (3, 4), (5, 6, 7))
RING = 8

SHIFTS = {
    "fx+": ("gx", 1, 1, 16), "fx-": ("gx", -1, 1, 16),
    "fz+": ("gz", 1, 1, 16), "fz-": ("gz", -1, 1, 16),
    "fy+": ("gy", 1, 1, 16), "fy-": ("gy", -1, 1, 16),
    "x0+": ("gx", 1, 8, 8), "x0-": ("gx", -1, 8, 8),
    "x1+": ("gx", 1, 12, 8), "x1-": ("gx", -1, 12, 8),
    "x2+1": ("gx", 1, 3, 8), "x2-1": ("gx", -1, 3, 8),
    "x2+2": ("gx", 2, 3, 8), "x2-2": ("gx", -2, 3, 8),
    "z0+": ("gz", 1, 4, 24), "z0-": ("gz", -1, 4, 24),
    "z1+": ("gz", 1, 7, 24), "z1-": ("gz", -1, 7, 24),
    "z2+1": ("gz", 1, 3, 16), "z2-1": ("gz", -1, 3, 16),
    "z2+2": ("gz", 2, 1, 16), "z2-2": ("gz", -2, 1, 16),
    "y0+": ("gy", 1, 1, 24), "y0-": ("gy", -1, 1, 24),
    "y1+": ("gy", 1, 2, 24), "y1-": ("gy", -1, 2, 24),
    "y2+": ("gy", 1, 1, 16), "y2-": ("gy", -1, 1, 16),
    "y3+": ("gy", 1, 1, 16), "y3-": ("gy", -1, 1, 16),
}
GATHERS = {"gx3": ("gx", 8), "gz3": ("gz", 16), "gy4": ("gy", 8)}


KEPT = {
    "s0": (16, 16, 128), "p0": (20, 24, 256), "u1": (12, 24, 128), "p1": (14, 24, 128),
    "u2": (8, 16, 128), "p2": (10, 16, 128), "u3": (1, 16, 512), "p3": (1, 16, 512),
}
MATRICES = {
    "lanes3": (512, 128), "lanes4": (128, 128), "up5": (128, 128), "up4": (128, 128), "up3": (128, 128),
    "up2": (128, 128), "up1": (128, 256), "next3": (128, 128), "next2": (128, 128), "next1": (128, 256),
    "block4": (128, 128), "block3": (192, 128), "block2": (384, 128), "block1": (576, 384),
}


def iota(shape, dim):
    return lax.broadcasted_iota(jnp.int32, shape, dim)


def number(cond):
    return jnp.where(cond, 1.0, 0.0).astype(jnp.float32)


def parts_of(v):
    high = v.astype(jnp.bfloat16)
    return high, (v - high.astype(jnp.float32)).astype(jnp.bfloat16)


def product(a, b):
    return jnp.dot(a, b, preferred_element_type=jnp.float32)


def times(v, matrix):
    high, low = parts_of(v)
    if v.shape[1] == LANES:
        return product(jnp.concatenate([high, low], axis=1), jnp.concatenate([matrix, matrix], axis=0))
    return product(high, matrix) + product(low, matrix)


def onto(matrix, v):
    high, low = parts_of(v)
    if v.shape[1] == LANES:
        both = product(matrix, jnp.concatenate([high, low], axis=1))
        return both[:, :LANES] + both[:, LANES:]
    return product(matrix, high) + product(matrix, low)


def select_matrix(shape, hit, value=1.0):
    return jnp.where(hit(iota(shape, 0), iota(shape, 1)), value, 0.0).astype(jnp.bfloat16)


def rows_of(stacked, rows):
    return [stacked[i * rows:(i + 1) * rows] for i in range(stacked.shape[0] // rows)]


def lanes_of(stacked):
    return [stacked[:, i * LANES:(i + 1) * LANES] for i in range(stacked.shape[1] // LANES)]


def right(planes, matrix):
    return rows_of(times(jnp.concatenate(planes, axis=0), matrix), planes[0].shape[0])


def left(matrix, planes):
    return lanes_of(onto(matrix, jnp.concatenate(planes, axis=1)))


def twice(matrix):
    return jnp.concatenate([matrix, matrix], axis=0)


def spread_rows(planes, block):
    stacked = jnp.concatenate(planes, axis=0)
    missing = block.shape[1] - stacked.shape[0]
    if missing:
        stacked = jnp.concatenate([stacked, jnp.zeros((missing, LANES), jnp.float32)], axis=0)
    return product(block, jnp.concatenate(parts_of(stacked), axis=1)).astype(jnp.bfloat16)


def widen(planes, rows, block, up, following):
    both = spread_rows(planes, block)
    half = both.shape[0] // 2
    own, beside = both[:half], both[half:]
    outer = product(beside, twice(up)) + product(own, twice(following))
    return rows_of(product(own, twice(up)), rows), rows_of(outer, rows)


def total(terms):
    terms = [t for t in terms if t is not None]
    out = terms[0]
    for t in terms[1:]:
        out = out + t
    return out


class Field:
    def __init__(self, lo, hi, make):
        self.lo, self.hi, self.make, self.have = lo, hi, make, {}

    def __call__(self, z):
        if z < self.lo or z > self.hi:
            return None
        if z not in self.have:
            self.have[z] = self.make(z)
        return self.have[z]


def field_of(lo, planes):
    return Field(lo, lo + len(planes) - 1, lambda z: planes[z - lo])


class Math:
    def __init__(self, env):
        self.env = env
        self.iz, self.ix, self.iy = env.position

    def roll(self, v, shift, axis):
        shift = shift % v.shape[axis]
        return v if shift == 0 else self.env.roll(v, shift, axis)

    def place_rows(self, v, at, rows):
        pad = jnp.zeros((rows - v.shape[0],) + v.shape[1:], v.dtype)
        return self.roll(jnp.concatenate([v, pad], axis=0), at, 0)

    def take_rows(self, v, at, rows):
        return self.roll(v, -at, 0)[:rows]

    def mask(self, level, rows, row_off, lanes, own_y):
        nz, nx, ny = 16 >> level, 16 >> level, 128 >> level
        x = iota((rows, lanes), 0) - row_off + self.ix * nx
        lane = iota((rows, lanes), 1)
        y = jnp.where(lane < (own_y + lanes) // 2, lane, lane - lanes) + self.iy * ny
        flat = number((x >= 0) & (x < 128 >> level) & (y >= 0) & (y < 1024 >> level))

        def make(z):
            if 0 <= z < nz:
                return flat
            at = self.iz * nz + z
            return flat * number((at >= 0) & (at < 128 >> level))

        return Field(-16, 32, make)

    def beside(self, f, z):
        v = f(z)
        terms = [f(z - 1), f(z + 1)]
        if v is not None:
            terms += [self.roll(v, 1, 0), self.roll(v, -1, 0), self.roll(v, 1, 1), self.roll(v, -1, 1)]
        return total(terms)

    def correction(self, r, mask, lo, hi):
        def make(z):
            v = r(z)
            near = BETA * self.beside(r, z)
            return mask(z) * (near if v is None else OWN * v + near)
        return Field(lo, hi, make)

    def minus_op(self, b, x, mask, lo, hi):
        def make(z):
            out = self.beside(x, z)
            if x(z) is not None:
                out = out - 6.0 * x(z)
            if b(z) is not None:
                out = out + b(z)
            return out if mask is None else mask(z) * out
        return Field(lo, hi, make)

    def minus_op_of_coarse(self, b, inner, outer, lo_coarse, mask, lo, hi):
        def make(z):
            at = (z >> 1) - lo_coarse
            return mask(z) * (b(z) + outer[at] + inner[at + 2 * (z & 1) - 1] - 3.0 * inner[at])
        return Field(lo, hi, make)

    def slots(self, rows, start, width):
        lane = (iota((rows, LANES), 1) - start) & (LANES - 1)
        return number(lane < width)

    def pack(self, planes, start, width=8):
        rows, per = planes[0].shape[0], LANES // width
        tiles = []
        for g in range(0, len(planes), per):
            tiles.append(total([
                self.slots(rows, width * w, width) * self.roll(plane, width * w - start, 1)
                for w, plane in enumerate(planes[g:g + per])
            ]))
        return tiles

    def unpack(self, tiles, count, start, width=8):
        keep, per = self.slots(tiles[0].shape[0], start, width), LANES // width
        return [keep * self.roll(tiles[i // per], start - width * (i % per), 1) for i in range(count)]


class Selections:
    def __init__(self, ix, iy):
        self.lanes0 = select_matrix((256, 128), lambda a, c: (a >> 1) == c, 0.5)
        self.rows0 = select_matrix((16, 24), lambda a, c: (c >> 1) + 2 == a)
        self.lanes1 = select_matrix((128, 128), lambda a, c: (a >> 1) + jnp.where(a >= 96, 64, 0) == c, 0.5)
        self.halve_rows = select_matrix((8, 16), lambda a, c: (c >> 1) == a)
        self.lanes2 = select_matrix((128, 128), lambda a, c: (jnp.where(a < 80, a, a - 128) >> 1) + 2 == c, 0.5)
        self.ix, self.iy = ix, iy

    def small(self, env):
        self.env = env
        self.rows4 = select_matrix((16, 32), lambda a, c: (c >> 3) * 4 + ((c & 7) >> 1) == a)
        self.up_rows5 = select_matrix((32, 16), lambda a, c: (a >> 3) * 4 + ((a & 7) >> 1) == c)

    def rest(self, env):
        ix, iy = self.ix, self.iy
        y_of = lambda c: jnp.where(c < 80, c, c - 128)
        y_fine = lambda c: jnp.where(c < 96, c, c - 128)
        side = lambda c: 2 * (c & 1) - 1

        def blocks(rows, depth, count, coarse, kinds=2):
            shape = (rows, -(-count * depth // LANES) * LANES)
            fine, column = iota(shape, 0), iota(shape, 1)
            out = []
            for kind in range(kinds):
                want = coarse(fine) + kind * side(fine)
                gap = column - jnp.where((want >= 0) & (want < depth), want, 4096)
                out += [number(gap == depth * k) for k in range(count)]
            return jnp.concatenate(out, axis=0).astype(jnp.bfloat16)

        env.keep_matrix("block4", blocks(16, 8, 8, lambda a: a >> 1, 1))
        env.keep_matrix("block3", blocks(16, 16, 6, lambda a: 2 * ix + ((a - 6) >> 1)))
        env.keep_matrix("block2", blocks(24, 16, 8, lambda a: (a >> 1) + 2))
        env.keep_matrix("block1", blocks(24, 24, 12, lambda a: ((a - 4) >> 1) + 8))
        hits = {
            "lanes3": lambda a, c: 16 * (a >> 6) + ((a & 31) >> 1) == c,
            "lanes4": lambda a, c: ((a >> 1) == c) & (a < 64),
            "up5": lambda a, c: (a == (c >> 1)) & (c < 64),
            "up4": lambda a, c: (a == 8 * iy + (((c & 31) - 8) >> 1)) & (c < 64),
            "up3": lambda a, c: (a - 8 == (y_of(c) >> 1)) & (a < 32) & (y_of(c) < 36) & (y_of(c) >= -4),
            "up2": lambda a, c: y_of(a) == (y_fine(c) >> 1),
            "up1": lambda a, c: a == (c >> 1),
            "next3": lambda a, c: (
                (a - 8 == (y_of(c) >> 1) + side(c)) & (a < 32) & (y_of(c) < 36) & (y_of(c) >= -4)),
            "next2": lambda a, c: y_of(a) == (y_fine(c) >> 1) + side(c),
            "next1": lambda a, c: a == (((c >> 1) + side(c)) & 127),
        }
        for name, hit in hits.items():
            value = 0.5 if name.startswith("lanes") else 1.0
            env.keep_matrix(name, select_matrix(MATRICES[name], hit, value))

    def kept(self, name):
        return self.env.matrix(name)


def cycle(env):
    m = Math(env)
    iz, ix, iy = env.position
    pick = Selections(ix, iy)
    x_own, b_own = env.load()
    zeros = lambda *s: jnp.zeros(s, jnp.float32)

    mask0 = m.mask(0, 24, 4, 256, 128)
    put0 = lambda v: jnp.concatenate([m.place_rows(v, 4, 24), zeros(24, LANES)], axis=1)
    xc = Field(0, 15, lambda z: put0(x_own[z]))
    bc = Field(0, 15, lambda z: put0(b_own[z]))
    r0 = m.minus_op(bc, xc, mask0, -1, 16)
    u0 = m.correction(r0, mask0, -2, 17)
    p0 = m.minus_op(r0, u0, None, -3, 18)
    coarse = [total([p0(2 * z), p0(2 * z + 1)]) for z in range(-2, 10)]
    coarse = right(coarse, pick.lanes0)
    coarse = left(pick.rows0, coarse)
    mask1c = m.mask(1, 16, 4, 128, 64)
    b1c = field_of(-2, [mask1c(z) * v for z, v in zip(range(-2, 10), coarse)])

    u1 = m.correction(b1c, mask1c, -3, 10)
    p1 = m.minus_op(b1c, u1, None, -4, 11)
    coarse = [total([p1(2 * z), p1(2 * z + 1)]) for z in range(-2, 6)]
    coarse = left(pick.halve_rows, right(coarse, pick.lanes1))
    mask2e = m.mask(2, 8, 2, 128, 32)
    b2c = [mask2e(z) * v for z, v in zip(range(-2, 6), coarse)]

    mask2c = m.mask(2, 16, 4, 128, 32)
    b2p = field_of(-2, [m.place_rows(v, 2, 16) for v in b2c])
    u2 = m.correction(b2p, mask2c, -3, 6)
    p2 = m.minus_op(b2p, u2, None, -4, 7)
    coarse = [total([p2(2 * z), p2(2 * z + 1)]) for z in range(-2, 4)]
    coarse = left(pick.halve_rows, right(coarse, pick.lanes2))
    b3c = total([m.roll(v, 20 * s, 1) for s, v in enumerate(coarse)])

    env.ready()
    env.gather_send("gx3", b3c)
    env.shift_send("fx+", [env.row(x_own, 15)])
    env.shift_send("fx-", [env.row(x_own, 0)])
    env.shift_send("fz+", [x_own[15]])
    env.shift_send("fz-", [x_own[0]])
    lane16 = iota((16, LANES), 1)
    env.shift_send("fy+", m.pack(x_own, 127, 1))
    env.shift_send("fy-", m.pack(x_own, 0, 1))
    packed2 = [total([m.roll(b2c[i], 40 * w + 2, 1) for w, i in enumerate(g)]) for g in GROUPS2]
    for d in (1, -1, 2, -2):
        env.shift_send("x2%+d" % d, packed2)
    env.shift_send("x1+", [m.take_rows(b1c(z), 7, 8) for z in range(-2, 10)])
    env.shift_send("x1-", [m.take_rows(b1c(z), 2, 8) for z in range(-2, 10)])

    row_a, lane_a = iota((16, LANES), 0), iota((16, LANES), 1)
    inside = lambda at: (number(at > 0), number(at < RING - 1))
    (z_lo, z_hi), (x_lo, x_hi), (y_lo, y_hi) = inside(iz), inside(ix), inside(iy)
    row_first, row_last = x_lo * number(row_a == 0), x_hi * number(row_a == 15)
    row_later, row_sooner = number(row_a > 0), number(row_a < 15)
    y_first, y_last = y_lo * number(lane_a == 0), y_hi * number(lane_a == 127)
    y_later, y_sooner = number(lane_a > 0), number(lane_a < 127)
    fx_lo, fx_hi = env.shift_recv("fx+")[0], env.shift_recv("fx-")[0]
    fz_lo, fz_hi = z_lo * env.shift_recv("fz+")[0], z_hi * env.shift_recv("fz-")[0]
    fy_lo, fy_hi = env.shift_recv("fy+")[0], env.shift_recv("fy-")[0]
    r_own = []
    for z in range(16):
        v = x_own[z]
        near = (x_own[z - 1] if z else fz_lo) + (x_own[z + 1] if z < 15 else fz_hi)
        near = near + row_later * m.roll(v, 1, 0) + row_first * fx_lo[z:z + 1]
        near = near + row_sooner * m.roll(v, -1, 0) + row_last * fx_hi[z:z + 1]
        near = near + y_later * m.roll(v, 1, 1) + y_first * m.roll(fy_lo, -z, 1)
        near = near + y_sooner * m.roll(v, -1, 1) + y_last * m.roll(fy_hi, 127 - z, 1)
        r_own.append(b_own[z] - 6.0 * v + near)
    row8 = iota((8, LANES), 0)
    is_low = row8 < 4
    two = lambda a, b: jnp.where(is_low, a, b)
    half = lambda v: m.roll(v, 4, 0)
    env.shift_send("x0+", [two(half(r_own[2 * i][8:]), r_own[2 * i + 1][8:]) for i in range(8)])
    env.shift_send("x0-", [two(r_own[2 * i][:8], half(r_own[2 * i + 1][:8])) for i in range(8)])

    pick.small(env)

    parts = env.gather_recv("gx3")
    wide = total([m.place_rows(v, 2 * k, 24) for k, v in enumerate(parts)])
    b3x = m.take_rows(wide, 2, 16)

    env.gather_send("gz3", b3x)
    env.region(lambda: pick.rest(env))

    before, after = env.shift_recv("x0+"), env.shift_recv("x0-")
    r0x = []
    for z in range(16):
        low, high = half(r_own[z][:8]), half(r_own[z][8:])
        lo, hi = before[z // 2], after[z // 2]
        if z % 2:
            lo = half(lo)
        else:
            hi = half(hi)
        r0x.append(jnp.concatenate([two(lo, low), two(low, high), two(high, hi)], axis=0))
    env.shift_send("z0+", r0x[12:])
    env.shift_send("z0-", r0x[:4])

    got = {d: env.shift_recv("x2%+d" % d) for d in (1, -1, 2, -2)}
    low, high = number(row8 < 4), number(row8 >= 4)
    b2x = []
    for i in range(3):
        lo = got[1][i] + low * half(got[2][i])
        hi = got[-1][i] + high * half(got[-2][i])
        b2x.append(jnp.concatenate([lo, hi], axis=0) + m.place_rows(packed2[i], 4, 16))
    env.shift_send("z2+1", b2x)
    env.shift_send("z2-1", b2x)
    env.shift_send("z2+2", b2x[2:])
    env.shift_send("z2-2", b2x[:1])

    before, after = env.shift_recv("x1+"), env.shift_recv("x1-")
    b1x = [
        m.place_rows(b1c(i - 2), 4, 24) + m.place_rows(before[i], 3, 24) + m.place_rows(after[i], 14, 24)
        for i in range(12)
    ]
    env.shift_send("z1+", b1x[5:])
    env.shift_send("z1-", b1x[:7])

    parts = env.gather_recv("gz3")
    lane = iota((16, LANES), 1)
    tiles = []
    for q in range(4):
        tile = None
        for w in range(4):
            z = 4 * q + w
            here = []
            for k in range(RING):
                s = z - 2 * k + 2
                if 0 <= s < 6:
                    here.append(m.roll(parts[k], 32 * w + 6 - 20 * s, 1))
            at = lane - (32 * w + 6)
            part = number((at >= 0) & (at < 20)) * total(here)
            tile = part if tile is None else tile + part
        tiles.append(tile)
    row16, lane512 = iota((16, 512), 0), iota((16, 512), 1)
    slot = lane512 & 31
    y3 = slot - 8 + 16 * iy
    mask3 = number((y3 >= 0) & (y3 < 128))
    not_first, not_last = number(row16 > 0), number(row16 < 15)
    not_bottom, not_top = number(lane512 >= 32), number(lane512 < 480)

    def beside3(v):
        out = not_first * m.roll(v, 1, 0) + not_last * m.roll(v, -1, 0)
        out = out + not_bottom * m.roll(v, 32, 1) + not_top * m.roll(v, -32, 1)
        return out + m.roll(v, 1, 1) + m.roll(v, -1, 1)

    correction3 = lambda r: mask3 * (OWN * r + BETA * beside3(r))
    minus_op3 = lambda b, x: mask3 * (b - 6.0 * x + beside3(x))

    b3s = mask3 * jnp.concatenate(tiles, axis=1)
    p3 = minus_op3(b3s, correction3(b3s))
    b4c = onto(pick.halve_rows, times(p3, pick.kept("lanes3")))

    env.gather_send("gy4", b4c)
    octet = (lane >> 3) & 3
    squeeze = lambda at: total([
        number(octet == q) * m.roll(v, 8 * q - at, 1) for q, v in enumerate(lanes_of(b3s))
    ])
    env.shift_send("y3+", [squeeze(19)])
    env.shift_send("y3-", [squeeze(6)])

    r0w = env.shift_recv("z0+") + r0x + env.shift_recv("z0-")
    env.shift_send("y0+", m.pack(r0w, 124, 4))
    env.shift_send("y0-", m.pack(r0w, 0, 4))

    got = {d: env.shift_recv("z2%+d" % d) for d in (1, -1, 2, -2)}
    keep = m.slots(16, 126, 40)

    def plane2(groups, i):
        g = [i in group for group in GROUPS2].index(True)
        return m.roll(groups[g], -(40 * GROUPS2[g].index(i) + 2), 1)

    b2w = []
    for z in range(-5, 9):
        here = []
        if -2 <= z <= 5:
            here.append(plane2(b2x, z + 2))
        if z <= 1:
            here.append(plane2(got[1], z + 6))
        if z >= 2:
            here.append(plane2(got[-1], z - 2))
        if z <= -3:
            here.append(plane2([None, None] + got[2], z + 10))
        if z >= 6:
            here.append(plane2(got[-2], z - 6))
        b2w.append(keep * total(here))
    env.shift_send("y2+", m.pack(b2w, 27))
    env.shift_send("y2-", m.pack(b2w, 126))

    before, after = env.shift_recv("z1+"), env.shift_recv("z1-")
    b1w = []
    for z in range(-5, 13):
        here = []
        if -2 <= z <= 9:
            here.append(b1x[z + 2])
        if z <= 1:
            here.append(before[z + 5])
        if z >= 6:
            here.append(after[z - 6])
        b1w.append(total(here))
    env.shift_send("y1+", m.pack(b1w, 59))
    env.shift_send("y1-", m.pack(b1w, 126))

    kept = {}
    before0, after0 = env.shift_recv("y0+"), env.shift_recv("y0-")

    def finest():
        mask = m.mask(0, 24, 4, 256, 128)
        low, high = m.unpack(before0, 24, 124, 4), m.unpack(after0, 24, 0, 4)
        r = field_of(-4, [
            mask(i - 4) * jnp.concatenate([v, low[i] + high[i]], axis=1) for i, v in enumerate(r0w)
        ])
        u = m.correction(r, mask, -3, 18)
        kept["p0"] = env.keep("p0", -2, m.minus_op(r, u, None, -2, 17))
        near_x = Field(0, 15, lambda z: x_own[z] + m.take_rows(u(z)[:, :LANES], 4, 16))
        kept["s0"] = env.keep("s0", 0, near_x)

    env.region(finest)

    mask0 = m.mask(0, 24, 4, 256, 128)
    mask1 = m.mask(1, 24, 8, LANES, 64)
    mask2 = m.mask(2, 16, 6, LANES, 32)
    env.flush()

    parts = env.gather_recv("gy4")
    row, lane = iota((8, LANES), 0), iota((8, LANES), 1)
    keep = []
    for j in range(RING):
        at = lane - (8 * j - 4)
        keep.append(number((at >= 0) & (at < 16) & (lane < 64)))
    b4 = field_of(0, [
        total([keep[j] * m.roll(parts[j], 8 * j - 4 - 16 * z, 1) for j in range(RING)]) for z in range(8)
    ])
    mask4 = number(lane < 64)
    first8, last8 = number(row > 0), number(row < 7)

    def beside4(f, z):
        v = f(z)
        return total([
            f(z - 1), f(z + 1), first8 * m.roll(v, 1, 0), last8 * m.roll(v, -1, 0), m.roll(v, 1, 1), m.roll(v, -1, 1)
        ])

    def correction4(r):
        return Field(0, 7, lambda z: mask4 * (OWN * r(z) + BETA * beside4(r, z)))

    def minus_op4(b, x):
        return Field(0, 7, lambda z: mask4 * (b(z) - 6.0 * x(z) + beside4(x, z)))

    u4 = correction4(b4)
    p4 = minus_op4(b4, u4)
    coarse = jnp.concatenate([p4(2 * z) + p4(2 * z + 1) for z in range(4)], axis=0)
    b5 = onto(pick.rows4, times(coarse, pick.kept("lanes4")))

    row, lane = iota((16, LANES), 0), iota((16, LANES), 1)
    mask5 = number(lane < 32)
    first5, last5 = number((row & 3) > 0), number((row & 3) < 3)
    bottom5, top5 = number(row >= 4), number(row < 12)

    def beside5(v):
        out = first5 * m.roll(v, 1, 0) + last5 * m.roll(v, -1, 0)
        out = out + bottom5 * m.roll(v, 4, 0) + top5 * m.roll(v, -4, 0)
        return out + m.roll(v, 1, 1) + m.roll(v, -1, 1)

    u5 = mask5 * (OWN * b5 + BETA * beside5(b5))
    p5 = mask5 * (b5 - 6.0 * u5 + beside5(u5))
    e5 = u5 + mask5 * (OWN * p5 + BETA * beside5(p5))
    env.coarse_out(e5)

    sides = {tag: (env.shift_recv(tag + "+"), env.shift_recv(tag + "-")) for tag in ("y3", "y2", "y1")}

    def window(level, planes, tag, rows, row_off, lo, own_y, at_low, at_high):
        mask = m.mask(level, rows, row_off, LANES, own_y)
        before = m.unpack(sides[tag][0], len(planes), at_low)
        after = m.unpack(sides[tag][1], len(planes), at_high)
        return mask, field_of(lo, [
            mask(lo + i) * (v + before[i] + after[i]) for i, v in enumerate(planes)
        ])

    def coarser():
        before, after = sides["y3"][0][0], sides["y3"][1][0]
        slot16 = lane16 & 31
        low_slot, high_slot = number((slot16 >= 3) & (slot16 < 11)), number((slot16 >= 22) & (slot16 < 30))
        b = mask3 * (b3s + jnp.concatenate([
            low_slot * m.roll(before, 3 - 8 * q, 1) + high_slot * m.roll(after, 22 - 8 * q, 1) for q in range(4)
        ], axis=1))
        u = correction3(b)
        kept["u3"], kept["p3"] = env.keep("u3", 0, lambda z: u), env.keep("p3", 0, lambda z: minus_op3(b, u))
        mask, b2 = window(2, b2w, "y2", 16, 6, -5, 32, 123, 30)
        u2 = m.correction(b2, mask, -4, 7)
        kept["p2"] = env.keep("p2", -3, m.minus_op(b2, u2, None, -3, 6))
        kept["u2"] = env.keep("u2", -2, u2)
        mask, b1 = window(1, b1w, "y1", 24, 8, -5, 64, 123, 62)
        u1 = m.correction(b1, mask, -4, 11)
        kept["p1"] = env.keep("p1", -3, m.minus_op(b1, u1, None, -3, 10))
        kept["u1"] = env.keep("u1", -2, u1)

    coarser()
    s0, u1, u2, u3, p3 = (kept[name] for name in ("s0", "u1", "u2", "u3", "p3"))
    p0, p1, p2 = Field(-2, 17, kept["p0"]), Field(-3, 10, kept["p1"]), Field(-3, 6, kept["p2"])

    wide = product(spread_rows([e5], pick.up_rows5), twice(pick.kept("up5")))
    c4 = rows_of(wide, 8)
    c4 = field_of(0, [c4[z // 2] for z in range(8)])
    q4 = minus_op4(p4, c4)
    v4 = correction4(q4)
    e4 = [u4(z) + c4(z) + v4(z) for z in range(8)]

    planes = rows_of(product(spread_rows(e4, pick.kept("block4")), twice(pick.kept("up4"))), 16)
    c3 = mask3 * jnp.concatenate([planes[2 * k] + m.roll(planes[2 * k + 1], 64, 1) for k in range(4)], axis=1)
    e3 = u3(0) + c3 + correction3(minus_op3(p3(0), c3))

    tiles = lanes_of(e3)
    near = env.window([m.roll(tiles[z // 4], -32 * (z % 4), 1) for z in range(16)])
    inner2, outer2 = widen(near, 16, pick.kept("block3"), pick.kept("up3"), pick.kept("next3"))

    v2 = m.correction(m.minus_op_of_coarse(p2, inner2, outer2, -2, mask2, -3, 6), mask2, -2, 5)
    e2 = [u2(z) + inner2[(z >> 1) + 2] + v2(z) for z in range(-2, 6)]

    inner1, outer1 = widen(e2, 24, pick.kept("block2"), pick.kept("up2"), pick.kept("next2"))
    v1 = m.correction(m.minus_op_of_coarse(p1, inner1, outer1, -2, mask1, -3, 10), mask1, -2, 9)
    e1 = [u1(z) + inner1[(z >> 1) + 2] + v1(z) for z in range(-2, 10)]

    inner0, outer0 = widen(e1, 24, pick.kept("block1"), pick.kept("up1"), pick.kept("next1"))
    q0 = m.minus_op_of_coarse(p0, inner0, outer0, -2, mask0, -2, 17)
    v0 = m.correction(q0, mask0, -1, 16)
    left_over = m.minus_op(q0, v0, None, 0, 15)
    inner = lambda v: m.take_rows(v[:, :LANES], 4, 16)
    for z in range(16):
        env.fine_out(z, s0(z) + inner(inner0[(z >> 1) + 2] + v0(z)), inner(left_over(z)))


class KernelEnv:
    def __init__(self, refs):
        self.refs = refs
        self.position = tuple(lax.axis_index(a) for a in ("gz", "gx", "gy"))
        self.at = dict(zip(("gz", "gx", "gy"), self.position))
        self.started = []
        self.loads = [
            pltpu.make_async_copy(refs["x_in"], refs["previous"], refs["load_sems"].at[0]),
            pltpu.make_async_copy(refs["b_in"], refs["divergence"], refs["load_sems"].at[1]),
        ]
        self.barrier = pltpu.get_barrier_semaphore()
        for d in (4, 3, 5, 2, 6, 1, 7):
            for axis in ("gx", "gy", "gz"):
                pl.semaphore_signal(
                    self.barrier, inc=1, device_id={axis: self.peer(axis, d)}, device_id_type=pl.DeviceIdType.MESH)
            if d == 4:
                for load in self.loads:
                    load.start()

    def peer(self, axis, d):
        return lax.rem(self.at[axis] + (d + RING), RING)

    def roll(self, v, shift, axis):
        return pltpu.roll(v, shift, axis)

    def load(self):
        for load in self.loads:
            load.wait()
        return [[self.refs[n][16 * z:16 * z + 16] for z in range(16)] for n in ("previous", "divergence")]

    def row(self, planes, x):
        return self.refs["previous"][pl.ds(x, 16, stride=16), :]

    def ready(self):
        pl.semaphore_wait(self.barrier, 3 * (RING - 1))

    def copy(self, src, dst, send_sem, recv_sem, axis, d):
        return pltpu.make_async_remote_copy(
            src_ref=src, dst_ref=dst, send_sem=send_sem, recv_sem=recv_sem,
            device_id={axis: self.peer(axis, d)}, device_id_type=pl.DeviceIdType.MESH)

    def shift_copy(self, name):
        axis, d, _, _ = SHIFTS[name]
        i = list(SHIFTS).index(name)
        return self.copy(
            self.refs["out" + name], self.refs["in" + name], self.refs["shift_sems"].at[0, i],
            self.refs["shift_sems"].at[1, i], axis, d)

    def shift_send(self, name, planes):
        ref = self.refs["out" + name]
        for i, v in enumerate(planes):
            ref[i] = v
        copy = self.shift_copy(name)
        copy.start()
        self.started.append(copy)

    def shift_recv(self, name):
        self.shift_copy(name).wait_recv()
        ref = self.refs["in" + name]
        return [ref[i] for i in range(SHIFTS[name][2])]

    def gather_send(self, name, v):
        axis, _ = GATHERS[name]
        i = list(GATHERS).index(name)
        me = self.at[axis]
        buf, src, sems = self.refs["in" + name], self.refs["out" + name], self.refs["gather_sems"]
        src[...] = v
        for d in (4, 3, 5, 2, 6, 1, 7):
            copy = self.copy(src, buf.at[me], sems.at[0, i, d], sems.at[1, i, me], axis, d)
            copy.start()
            self.started.append(copy)
        buf[me] = v

    def gather_recv(self, name):
        axis, _ = GATHERS[name]
        i = list(GATHERS).index(name)
        buf, src, sems = self.refs["in" + name], self.refs["out" + name], self.refs["gather_sems"]
        for d in range(1, RING):
            k = self.peer(axis, d)
            self.copy(src, buf.at[k], sems.at[0, i, d], sems.at[1, i, k], axis, d).wait_recv()
        return [buf[k] for k in range(RING)]

    def window(self, planes):
        ref = self.refs["planes3"]
        zero = jnp.zeros((16, LANES), jnp.float32)
        for z in (0, 1, 18, 19):
            ref[z] = zero
        for z, v in enumerate(planes):
            ref[z + 2] = v
        return [ref[2 * self.position[0] + s] for s in range(6)]

    def region(self, work):
        pl.when(self.position[0] < RING)(work)

    def keep(self, name, lo, field):
        ref = self.refs["kept_" + name]
        for i in range(KEPT[name][0]):
            ref[i] = field(lo + i)
        return lambda z: ref[z - lo]

    def keep_matrix(self, name, matrix):
        self.refs["matrix_" + name][...] = matrix

    def matrix(self, name):
        return self.refs["matrix_" + name][...]

    def coarse_out(self, v):
        for z in range(4):
            self.refs["coarse"][z] = v[4 * z:4 * z + 4, :32]

    def fine_out(self, z, pressure, residual):
        self.refs["pressure"][z] = pressure
        self.refs["residual"][z] = residual

    def flush(self):
        for copy in self.started:
            copy.wait_send()
        self.started = []


def scratch():
    shapes = {}
    for name, (_, _, count, rows) in SHIFTS.items():
        shapes["out" + name] = pltpu.VMEM((count, rows, LANES), jnp.float32)
        shapes["in" + name] = pltpu.VMEM((count, rows, LANES), jnp.float32)
    for name, (_, rows) in GATHERS.items():
        shapes["out" + name] = pltpu.VMEM((rows, LANES), jnp.float32)
        shapes["in" + name] = pltpu.VMEM((RING, rows, LANES), jnp.float32)
    for name, shape in KEPT.items():
        shapes["kept_" + name] = pltpu.VMEM(shape, jnp.float32)
    for name, shape in MATRICES.items():
        shapes["matrix_" + name] = pltpu.VMEM(shape, jnp.bfloat16)
    shapes["previous"] = pltpu.VMEM((256, LANES), jnp.float32)
    shapes["divergence"] = pltpu.VMEM((256, LANES), jnp.float32)
    shapes["load_sems"] = pltpu.SemaphoreType.DMA((2,))
    shapes["planes3"] = pltpu.VMEM((20, 16, LANES), jnp.float32)
    shapes["shift_sems"] = pltpu.SemaphoreType.DMA((2, len(SHIFTS)))
    shapes["gather_sems"] = pltpu.SemaphoreType.DMA((2, len(GATHERS), RING))
    return shapes


def kernel(names, divergence, previous, pressure, residual, coarse, *buffers):
    refs = dict(zip(names, buffers), x_in=previous, b_in=divergence, pressure=pressure, residual=residual, coarse=coarse)
    env = KernelEnv(refs)
    cycle(env)
    env.flush()


def store_kernel(*refs):
    values, outs, sems = refs[:3], refs[3:6], refs[6]
    copies = [pltpu.make_async_copy(v, o, sems.at[i]) for i, (v, o) in enumerate(zip(values, outs))]
    for copy in copies:
        copy.start()
    for copy in copies:
        copy.wait()


def body(divergence, pressure_prev):
    shapes = scratch()
    block = jax.ShapeDtypeStruct((16, 16, 128), jnp.float32)
    outs = (block, block, jax.ShapeDtypeStruct((4, 4, 32), jnp.float32))
    vmem, hbm = pl.BlockSpec(memory_space=pltpu.VMEM), pl.BlockSpec(memory_space=pltpu.HBM)
    results = pl.pallas_call(
        functools.partial(kernel, tuple(shapes)),
        out_shape=outs,
        in_specs=[hbm, hbm],
        out_specs=(vmem, vmem, vmem),
        scratch_shapes=list(shapes.values()),
        compiler_params=pltpu.CompilerParams(
            collective_id=0, has_side_effects=True, vmem_limit_bytes=48 * 1024 * 1024),
        name="cycle",
    )(*(pltpu.with_memory_space_constraint(v.reshape(256, 128), pltpu.HBM) for v in (divergence, pressure_prev)))
    return pl.pallas_call(
        store_kernel,
        out_shape=outs,
        in_specs=[vmem, vmem, vmem],
        out_specs=(hbm, hbm, hbm),
        scratch_shapes=[pltpu.SemaphoreType.DMA((3,))],
        compiler_params=pltpu.CompilerParams(vmem_limit_bytes=1024 * 1024),
        name="store",
    )(*results)


def solution(mesh):
    in_specs = (P("gz", "gx", "gy"), P("gz", "gx", "gy"))
    out_specs = (P("gz", "gx", "gy"), P("gz", "gx", "gy"), P())
    return jax.shard_map(body, mesh=mesh, in_specs=in_specs, out_specs=out_specs, check_vma=False)
```
